256 devices in a mesh: src: 16 (over y, z_hi, core), tgt: 16 (over z_lo, x).
Axes of the slice: x: 4, y: 4, z: 8 (z_hi: 2, z_lo: 4; z = z_hi * 4 + z_lo), core: 2. Of those that a mesh axis runs over, the one named last changes fastest.
Arguments:
- source_points: float32 [64, 65536], P(None, ('src', 'tgt')), may hold values from -1.5 to 1.5
- target_points: float32 [64, 65536], P(None, ('src', 'tgt')), may hold values from -1.5 to 1.5
- source_logw: float32 [65536], P(('src', 'tgt')), may hold values from -2 to 2
- target_logw: float32 [65536], P(('src', 'tgt')), may hold values from -2 to 2
- potential_in: float32 [65536], P(('src', 'tgt')), may hold values from -5 to 61
- pair_list: int32 [256, 128, 2], P(('src', 'tgt')), may hold values from 0 to 255, as said below
- pair_counts: int32 [256], P(('src', 'tgt')), may hold values from 16 to 128, as said below
Outputs:
- source_potential: float32 [65536], P(('src', 'tgt'))
- target_potential: float32 [65536], P(('src', 'tgt'))
The draws below stay inside these ranges and needn't reach their ends.
Inputs may be any that keep to these rules, and one draw needn't show every extreme that they name: `pair_list`: for row d = s * 16 + t, every source block lies in s * 16 to s * 16 + 15 and every target block equals t modulo 16; the entries of a row are distinct; only the first pair_counts[d] are live, later ones are ignored. Every source block and every target block whose ranges a row covers appears in a live pair of that row. `pair_counts`: some row has exactly 128 live pairs.
All inputs are finite; a program needn't handle non-finite values.
Results may differ from the reference program's by a relative error of at most 0.0003.
Values sent between devices are 32-bit elements; how exact they have to be, the bound alone decides.
No kernel may reach another device: no remote copies, remote signals or barrier semaphores. Data moves between devices by JAX's collectives and lax.ppermute only.
A program may use at most 64 MiB of HBM per device.

```python
import jax
import jax.numpy as jnp
from jax import lax

FEAT = 64
BLOCK = 256
BLOCKS = 256
TILES = 256
SLOTS = 128
NS = 65536
NT = 65536
N_SRC = 16
N_TGT = 16


def pair_tables(key):
    rows_tile = N_TGT
    cols_tile = N_SRC
    spots = rows_tile * cols_tile
    key_list = jax.random.fold_in(key, 101)
    key_count = jax.random.fold_in(key, 202)
    key_force = jax.random.fold_in(key, 303)
    index_all = jnp.arange(spots, dtype=jnp.int32)
    local_row = index_all // cols_tile
    local_col = index_all % cols_tile
    if rows_tile >= cols_tile:
        base_mask = local_col == local_row % cols_tile
    else:
        base_mask = local_row == local_col % rows_tile

    def one_tile(tile_key, tile_id):
        group_id = tile_id // N_TGT
        column_id = tile_id % N_TGT
        ranking = jax.random.permutation(tile_key, spots).astype(jnp.int32)
        priority = jnp.where(base_mask, ranking + spots, ranking)
        _, order = lax.top_k(priority, SLOTS)
        source_block = group_id * N_TGT + local_row[order]
        target_block = local_col[order] * N_TGT + column_id
        return jnp.stack([source_block, target_block], axis=-1).astype(jnp.int32)
    tile_keys = jax.random.split(key_list, TILES)
    lists = jax.vmap(one_tile)(tile_keys, jnp.arange(TILES, dtype=jnp.int32))
    factors = jax.random.randint(key_count, (2, TILES), 0, SLOTS)
    divisor = max(1, SLOTS * 3 // 4)
    base_count = max(rows_tile, cols_tile)
    counts_all = jnp.minimum(SLOTS, base_count + factors[0] * factors[1] // divisor)
    forced = jax.random.randint(key_force, (), 0, TILES)
    counts_all = jnp.where(jnp.arange(TILES) == forced, SLOTS, counts_all).astype(jnp.int32)
    return (lists, counts_all)


def draw_pair_list(key, part):
    lists, _ = pair_tables(key)
    return lists


def draw_pair_counts(key, part):
    _, counts_all = pair_tables(key)
    return counts_all


def draw_potential_in(key, part):
    key = jax.random.fold_in(key, 7)
    key_base = jax.random.fold_in(key, 0)
    return jnp.clip(jax.random.normal(key_base, (NT,)), -5.0, 5.0).astype(jnp.float32)


def shard_levels(own_key, extent, pieces, low, top_value):
    def one(position, shards_of):
        draws = jax.random.uniform(jax.random.fold_in(jax.random.fold_in(own_key, 6), position), (shards_of,), jnp.float32, low / len(pieces), top_value / len(pieces))
        return jnp.repeat(jnp.exp(draws), extent[position] // shards_of).reshape((-1,) + (1,) * (len(extent) - position - 1))

    loudness = one(*pieces[0])
    for cut in pieces[1:]:
        loudness = loudness * one(*cut)
    return loudness


def scatter_about(stream_key, shape, width, most, cuts=(), kind=jnp.bfloat16):
    array = width * jax.random.normal(stream_key, shape, jnp.float32)
    if cuts:
        array = array * shard_levels(stream_key, shape, cuts, -0.22, 0.18)
    return jnp.clip(array, -most, most).astype(kind)


def setup_inputs(seed: int = 0) -> dict:
    streams_of = jax.random.split(jax.random.key(seed), 8)
    source_points = scatter_about(streams_of[0], (FEAT, NS), 0.25, 1.5, ((1, 256),), jnp.float32)
    target_points = scatter_about(streams_of[1], (FEAT, NT), 0.25, 1.5, ((1, 256),), jnp.float32)
    source_logw = jnp.clip(jax.random.uniform(streams_of[2], (NS,), jnp.float32, -2.0, 2.0) * shard_levels(streams_of[2], (NS,), ((0, 256),), -0.4, 0.0), -2.0, 2.0)
    target_logw = jnp.clip(jax.random.uniform(streams_of[3], (NT,), jnp.float32, -2.0, 2.0) * shard_levels(streams_of[3], (NT,), ((0, 256),), -0.4, 0.0), -2.0, 2.0)
    potential_in = draw_potential_in(jax.random.fold_in(streams_of[7], 71), 0)
    pair_list = draw_pair_list(jax.random.fold_in(streams_of[7], 71), 0)
    pair_counts = draw_pair_counts(jax.random.fold_in(streams_of[7], 71), 0)
    return {"source_points": source_points, "target_points": target_points, "source_logw": source_logw, "target_logw": target_logw, "potential_in": potential_in, "pair_list": pair_list, "pair_counts": pair_counts}


epsilon = 0.25
lowest_log = -1.0e30


def merge_pair(first, second):
    highest = jnp.maximum(first[0], second[0])
    summed = first[1] * jnp.exp(first[0] - highest) + second[1] * jnp.exp(second[0] - highest)
    return highest, summed


def reference(source_points, target_points, source_logw, target_logw, potential_in, pair_list, pair_counts):
    xs = source_points.reshape(FEAT, BLOCKS, BLOCK).transpose(1, 0, 2)
    ys = target_points.reshape(FEAT, BLOCKS, BLOCK).transpose(1, 0, 2)
    xsq = jnp.sum(xs * xs, axis=1)
    ysq = jnp.sum(ys * ys, axis=1)
    flat_pairs = pair_list.reshape(-1, 2)
    alive_all = (jnp.arange(SLOTS)[None, :] < pair_counts[:, None]).reshape(-1)
    g_blocks = potential_in.reshape(BLOCKS, BLOCK)

    def tile_cost(sblk, tblk):
        inner_prod = jnp.dot(xs[sblk].T, ys[tblk], precision=lax.Precision.HIGHEST, preferred_element_type=jnp.float32)
        return xsq[sblk][:, None] + ysq[tblk][None, :] - 2.0 * inner_prod

    start = (jnp.full((BLOCKS, BLOCK), lowest_log, dtype=jnp.float32), jnp.zeros((BLOCKS, BLOCK), dtype=jnp.float32))

    def row_step(carry, item):
        entry, alive = item

        def visit_pair(state):
            sblk = entry[0]
            tblk = entry[1]
            scores = (g_blocks[tblk][None, :] - tile_cost(sblk, tblk)) / epsilon
            highest = jnp.max(scores, axis=1)
            summed = jnp.sum(jnp.exp(scores - highest[:, None]), axis=1)
            new_high, new_sum = merge_pair((state[0][sblk], state[1][sblk]), (highest, summed))
            return (state[0].at[sblk].set(new_high), state[1].at[sblk].set(new_sum))

        return lax.cond(alive, visit_pair, lambda state: state, carry), None

    row_parts, _ = lax.scan(row_step, start, (flat_pairs, alive_all))
    source_potential = epsilon * source_logw - epsilon * (row_parts[0] + jnp.log(row_parts[1])).reshape(-1)
    f_blocks = source_potential.reshape(BLOCKS, BLOCK)

    def col_step(carry, item):
        entry, alive = item

        def visit_pair(state):
            sblk = entry[0]
            tblk = entry[1]
            scores = (f_blocks[sblk][:, None] - tile_cost(sblk, tblk)) / epsilon
            highest = jnp.max(scores, axis=0)
            summed = jnp.sum(jnp.exp(scores - highest[None, :]), axis=0)
            new_high, new_sum = merge_pair((state[0][tblk], state[1][tblk]), (highest, summed))
            return (state[0].at[tblk].set(new_high), state[1].at[tblk].set(new_sum))

        return lax.cond(alive, visit_pair, lambda state: state, carry), None

    col_parts, _ = lax.scan(col_step, start, (flat_pairs, alive_all))
    target_potential = epsilon * target_logw - epsilon * (col_parts[0] + jnp.log(col_parts[1])).reshape(-1)
    return source_potential, target_potential
```

```python
import functools

import jax
import jax.numpy as jnp
from jax import lax
from jax.experimental import pallas as pl
from jax.experimental.pallas import tpu as pltpu
from jax.sharding import PartitionSpec as P

epsilon = 0.25
lowest_log = -1e30
log2e = 1.4426950408889634
ln2 = 0.6931471805599453
SIDE = 16
BLOCK = 256
FEAT = 64
ROWS = 72
UNROLL = 4
vmem_bytes = 30 * 1024 * 1024


def merge_pair(first, second):
    highest = jnp.maximum(first[0], second[0])
    summed = first[1] * jnp.exp(first[0] - highest) + second[1] * jnp.exp(second[0] - highest)
    return (highest, summed)


def cross_cost(left_all, left_sq, row_id, right_all, right_sq, col_id, block_len):
    left_points = lax.dynamic_slice_in_dim(left_all, row_id * block_len, block_len, 1)
    right_points = lax.dynamic_slice_in_dim(right_all, col_id * block_len, block_len, 1)
    left_norm = lax.dynamic_slice_in_dim(left_sq, row_id * block_len, block_len, 0)
    right_norm = lax.dynamic_slice_in_dim(right_sq, col_id * block_len, block_len, 0)
    inner_prod = lax.dot_general(
        left_points,
        right_points,
        (((0,), (0,)), ((), ())),
        precision=lax.Precision.HIGHEST,
        preferred_element_type=jnp.float32,
    )
    return left_norm[:, None] + right_norm[None, :] - 2.0 * inner_prod


def fold_part(running, position, highest, summed):
    old_high = lax.dynamic_slice_in_dim(running[0], position, 1, 0)[0]
    old_sum = lax.dynamic_slice_in_dim(running[1], position, 1, 0)[0]
    new_high, new_sum = merge_pair((old_high, old_sum), (highest, summed))
    return (
        lax.dynamic_update_slice_in_dim(running[0], new_high[None, :], position, 0),
        lax.dynamic_update_slice_in_dim(running[1], new_sum[None, :], position, 0),
    )


def plain_form(
    source_points, target_points, source_logw, target_logw, potential_in, pair_list, pair_counts
):
    n_tgt = lax.axis_size("tgt")
    n_src = lax.axis_size("src")
    block_len = source_points.shape[1]
    group_points = lax.all_gather(source_points, "tgt", axis=1, tiled=True)
    group_logw = lax.all_gather(source_logw, "tgt", axis=0, tiled=True)
    column_points = lax.all_gather(target_points, "src", axis=1, tiled=True)
    column_g = lax.all_gather(potential_in, "src", axis=0, tiled=True)
    group_sq = jnp.sum(group_points * group_points, axis=0)
    column_sq = jnp.sum(column_points * column_points, axis=0)
    row_start = (
        jnp.full((n_tgt, block_len), lowest_log, dtype=jnp.float32),
        jnp.zeros((n_tgt, block_len), dtype=jnp.float32),
    )
    col_start = (
        jnp.full((n_src, block_len), lowest_log, dtype=jnp.float32),
        jnp.zeros((n_src, block_len), dtype=jnp.float32),
    )
    own_entries = pair_list[0]
    own_count = pair_counts[0]

    def row_visit_pair(slot_id, carry):
        row_id = own_entries[slot_id, 0] % n_tgt
        col_id = own_entries[slot_id, 1] // n_tgt
        tile_cost = cross_cost(
            group_points, group_sq, row_id, column_points, column_sq, col_id, block_len
        )
        g_piece = lax.dynamic_slice_in_dim(column_g, col_id * block_len, block_len, 0)
        scores = (g_piece[None, :] - tile_cost) / epsilon
        highest = jnp.max(scores, axis=1)
        summed = jnp.sum(jnp.exp(scores - highest[:, None]), axis=1)
        return fold_part(carry, row_id, highest, summed)

    row_parts = lax.fori_loop(0, own_count, row_visit_pair, row_start)
    row_high = lax.pmax(row_parts[0], "tgt")
    row_sum = lax.psum(row_parts[1] * jnp.exp(row_parts[0] - row_high), "tgt")
    f_group = epsilon * group_logw - epsilon * (row_high + jnp.log(row_sum)).reshape(-1)
    f_own = lax.dynamic_slice_in_dim(f_group, lax.axis_index("tgt") * block_len, block_len, 0)

    def col_visit_pair(slot_id, carry):
        row_id = own_entries[slot_id, 0] % n_tgt
        col_id = own_entries[slot_id, 1] // n_tgt
        tile_cost = cross_cost(
            group_points, group_sq, row_id, column_points, column_sq, col_id, block_len
        )
        f_piece = lax.dynamic_slice_in_dim(f_group, row_id * block_len, block_len, 0)
        scores = (f_piece[:, None] - tile_cost) / epsilon
        highest = jnp.max(scores, axis=0)
        summed = jnp.sum(jnp.exp(scores - highest[None, :]), axis=0)
        return fold_part(carry, col_id, highest, summed)

    col_parts = lax.fori_loop(0, own_count, col_visit_pair, col_start)
    col_high = lax.pmax(col_parts[0], "src")
    col_sum = lax.psum(col_parts[1] * jnp.exp(col_parts[0] - col_high), "src")
    own_high = lax.dynamic_slice_in_dim(col_high, lax.axis_index("src"), 1, 0)[0]
    own_sum = lax.dynamic_slice_in_dim(col_sum, lax.axis_index("src"), 1, 0)[0]
    g_own = epsilon * target_logw - epsilon * (own_high + jnp.log(own_sum))
    return (f_own, g_own)


def pack_kernel(x_ref, y_ref, lw_ref, g_ref, xp_ref, yp_ref, xsq_ref, ysq_ref):
    x = x_ref[...]
    y = y_ref[...]
    x_sq = jnp.sum(x * x, axis=0, keepdims=True)
    y_sq = jnp.sum(y * y, axis=0, keepdims=True)
    b = (4.0 * log2e) * (g_ref[...] - y_sq)
    row = lax.broadcasted_iota(jnp.int32, (8, BLOCK), 0)
    b_max = jnp.max(b, axis=1, keepdims=True)
    xp_ref[0:FEAT, :] = x
    xp_ref[FEAT:ROWS, :] = jnp.where(row == 0, lw_ref[...], b_max)
    yp_ref[0:FEAT, :] = y
    yp_ref[FEAT:ROWS, :] = jnp.broadcast_to(b, (8, BLOCK))
    xsq_ref[...] = x_sq
    ysq_ref[...] = y_sq


def pack(x, y, lw, g):
    return pl.pallas_call(
        pack_kernel,
        out_shape=(
            jax.ShapeDtypeStruct((ROWS, BLOCK), jnp.float32),
            jax.ShapeDtypeStruct((ROWS, BLOCK), jnp.float32),
            jax.ShapeDtypeStruct((1, BLOCK), jnp.float32),
            jax.ShapeDtypeStruct((1, BLOCK), jnp.float32),
        ),
        in_specs=[pl.BlockSpec(memory_space=pltpu.VMEM)] * 4,
        out_specs=[pl.BlockSpec(memory_space=pltpu.VMEM)] * 4,
        name="pack",
    )(x, y, lw.reshape(1, BLOCK), g.reshape(1, BLOCK))


def row_kernel(
    count_ref, row_ref, xat_ref, yat_ref, where_ref,
    x0, x1, x2, x3, y0, y1, y2, y3,
    s_ref, aux_ref, k_ref,
    xa, ya, ub, acc, peak,
):
    xs = (x0, x1, x2, x3)
    ys = (y0, y1, y2, y3)
    b_maxes = [xs[q][p, FEAT + 1 : FEAT + 2, :] for q in range(4) for p in range(4)]
    shift = functools.reduce(jnp.maximum, b_maxes)
    x_mean_sq = jnp.zeros((1, 1), jnp.float32)
    for q in range(4):
        for p in range(4):
            at = q * 4 + p
            x = xs[q][p, 0:FEAT, :]
            mean = jnp.sum(x, axis=1, keepdims=True) * (1.0 / BLOCK)
            x_mean_sq = jnp.maximum(x_mean_sq, jnp.sum(mean * mean, axis=0, keepdims=True))
            x = x * (8.0 * log2e)
            hi = x.astype(jnp.bfloat16)
            lo = (x - hi.astype(jnp.float32)).astype(jnp.bfloat16)
            xa[at, 0:64, :] = hi
            xa[at, 64:128, :] = lo
            xa[at, 128:192, :] = hi
            xa[at, 192:256, :] = lo
            aux_ref[pl.ds(where_ref[at], 1), :] = xs[q][p, FEAT : FEAT + 1, :]
    y_sq = jnp.zeros((1, BLOCK), jnp.float32)
    b_low = jnp.full((1, BLOCK), 1e30, jnp.float32)
    b_high = jnp.full((1, BLOCK), -1e30, jnp.float32)
    for q in range(4):
        for p in range(4):
            at = q * 4 + p
            y = ys[q][p, 0:FEAT, :]
            y_sq = jnp.maximum(y_sq, jnp.sum(y * y, axis=0, keepdims=True))
            b = ys[q][p, FEAT : FEAT + 1, :] - shift
            b_low = jnp.minimum(b_low, b)
            b_high = jnp.maximum(b_high, b)
            turned = jnp.concatenate([y, y], axis=0).T
            hi = turned.astype(jnp.bfloat16)
            lo = (turned - hi.astype(jnp.float32)).astype(jnp.bfloat16)
            ya[at, :, 0:128] = hi
            ya[at, :, 128:256] = lo
            ub[at] = jnp.exp2(jnp.broadcast_to(b, (128, BLOCK)).T)
    lean = (8.0 * log2e) * jnp.sqrt(x_mean_sq * jnp.max(y_sq, axis=1, keepdims=True))
    top = jnp.max(b_high, axis=1, keepdims=True)
    good = (
        (lean <= 24.0)
        & (jnp.min(b_low, axis=1, keepdims=True) - top >= -105.0)
        & (jnp.abs(top) <= 16.0)
    )
    aux_ref[16:17, :] = shift
    aux_ref[17:18, :] = jnp.broadcast_to(top, (1, BLOCK))
    aux_ref[18:19, :] = shift + top
    aux_ref[19:24, :] = jnp.zeros((5, BLOCK), jnp.float32)

    acc[...] = jnp.zeros_like(acc)
    peak[...] = jnp.zeros_like(peak)
    count = count_ref[0]

    def group(step, carry):
        for u in range(UNROLL):
            raw = step * UNROLL + u
            slot = jnp.minimum(raw, count - 1)
            xat = xat_ref[slot]
            yat = yat_ref[slot]
            scores = jnp.dot(ya[yat], xa[xat], preferred_element_type=jnp.float32)
            tile = jnp.exp2(scores)
            short = tile.astype(jnp.bfloat16)
            k_ref[raw] = short
            peak[...] = jnp.maximum(peak[...], jnp.max(short.reshape(16, 16, BLOCK), axis=0))
            weight = ub[yat]
            left = tile[:, 0:128] * weight
            right = tile[:, 128:256] * weight
            live = raw < count
            row = row_ref[slot]
            left = jnp.sum(left.reshape(32, 8, 128), axis=0)
            right = jnp.sum(right.reshape(32, 8, 128), axis=0)
            acc[row, :, 0:128] += jnp.where(live, left, 0.0)
            acc[row, :, 128:256] += jnp.where(live, right, 0.0)
        return carry

    lax.fori_loop(0, pl.cdiv(count, UNROLL), group, 0)
    total = jnp.sum(acc[...], axis=1)
    highest = jnp.max(peak[...].astype(jnp.float32), axis=0, keepdims=True)
    good = good & (jnp.max(highest, axis=1, keepdims=True) <= 1.3e36)
    s_ref[...] = jnp.where(good, total, jnp.nan)


def row_pass(count, row, xat, yat, where, xs, ys):
    smem = pl.BlockSpec(memory_space=pltpu.SMEM)
    vmem = pl.BlockSpec(memory_space=pltpu.VMEM)
    return pl.pallas_call(
        row_kernel,
        out_shape=(
            jax.ShapeDtypeStruct((SIDE, BLOCK), jnp.float32),
            jax.ShapeDtypeStruct((24, BLOCK), jnp.float32),
            pltpu.VMEM((128, BLOCK, BLOCK), jnp.bfloat16),
        ),
        in_specs=[smem] * 5 + [vmem] * 8,
        out_specs=[vmem] * 3,
        scratch_shapes=[
            pltpu.VMEM((SIDE, BLOCK, BLOCK), jnp.bfloat16),
            pltpu.VMEM((SIDE, BLOCK, BLOCK), jnp.bfloat16),
            pltpu.VMEM((SIDE, BLOCK, 128), jnp.float32),
            pltpu.VMEM((SIDE, 8, BLOCK), jnp.float32),
            pltpu.VMEM((16, BLOCK), jnp.bfloat16),
        ],
        compiler_params=pltpu.CompilerParams(vmem_limit_bytes=vmem_bytes),
        name="row_pass",
    )(count, row, xat, yat, where, *xs, *ys)


def col_kernel(
    count_ref, row_ref, col_ref, own_ref, s_ref, aux_ref, sq_ref, k_ref,
    f_ref, t_ref,
    vp, acc,
):
    own = own_ref[0]
    total = s_ref[...]
    logw = aux_ref[0:16, :]
    v = jnp.exp(logw) / total * jnp.exp2(aux_ref[17:18, :])
    fine = jnp.where((total >= 1.5e-11) & (total <= 4.3e12), 1.0, 0.0)
    fine = jnp.min(jnp.min(fine, axis=1, keepdims=True), axis=0, keepdims=True) > 0.5
    v = jnp.where(fine, v, jnp.nan)
    hi = v.astype(jnp.bfloat16)
    rest = v - hi.astype(jnp.float32)
    mid = rest.astype(jnp.bfloat16)
    low = (rest - mid.astype(jnp.float32)).astype(jnp.bfloat16)
    lane_row = lax.broadcasted_iota(jnp.int32, (16, BLOCK), 0)
    zero = jnp.zeros((16, BLOCK), jnp.float32)
    for r in range(SIDE):
        a = jnp.broadcast_to(hi[r : r + 1, :].astype(jnp.float32), (16, BLOCK))
        b = jnp.broadcast_to(mid[r : r + 1, :].astype(jnp.float32), (16, BLOCK))
        c = jnp.broadcast_to(low[r : r + 1, :].astype(jnp.float32), (16, BLOCK))
        both = jnp.where(lane_row == 0, a, jnp.where(lane_row == 1, b, jnp.where(lane_row == 2, c, zero)))
        vp[r] = both.astype(jnp.bfloat16)
    own_s = s_ref[pl.ds(own, 1), :]
    own_lw = aux_ref[pl.ds(own, 1), :]
    f_ref[...] = epsilon * own_lw - epsilon * (jnp.log(own_s) + ln2 * aux_ref[16:17, :]) + sq_ref[...]

    acc[...] = jnp.zeros_like(acc)
    count = count_ref[0]

    def group(step, carry):
        for u in range(UNROLL):
            raw = step * UNROLL + u
            slot = jnp.minimum(raw, count - 1)
            part = lax.dot_general(
                vp[row_ref[slot]], k_ref[slot], (((1,), (1,)), ((), ())),
                preferred_element_type=jnp.float32,
            )
            acc[col_ref[slot]] += jnp.where(raw < count, part, 0.0)
        return carry

    lax.fori_loop(0, pl.cdiv(count, UNROLL), group, 0)
    t_ref[...] = jnp.sum(acc[...], axis=1)


def col_pass(count, row, col, own, total, aux, sq, kernel_tiles):
    smem = pl.BlockSpec(memory_space=pltpu.SMEM)
    vmem = pl.BlockSpec(memory_space=pltpu.VMEM)
    return pl.pallas_call(
        col_kernel,
        out_shape=(
            jax.ShapeDtypeStruct((1, BLOCK), jnp.float32),
            jax.ShapeDtypeStruct((SIDE, BLOCK), jnp.float32),
        ),
        in_specs=[smem] * 4 + [vmem] * 4,
        out_specs=[vmem] * 2,
        scratch_shapes=[
            pltpu.VMEM((SIDE, 16, BLOCK), jnp.bfloat16),
            pltpu.VMEM((SIDE, 16, BLOCK), jnp.float32),
        ],
        compiler_params=pltpu.CompilerParams(vmem_limit_bytes=vmem_bytes),
        name="col_pass",
    )(count, row, col, own, total, aux, sq, kernel_tiles)


def ring(k):
    return [(i, (i // 4) * 4 + (i + k) % 4) for i in range(SIDE)]


def hop(k):
    return [(i, (i + 4 * k) % SIDE) for i in range(SIDE)]


def swap(bit):
    return [(i, i ^ bit) for i in range(SIDE)]


def fast_form(x, y, lw, g, entries, count, tgt_id, src_id):
    xp, yp, x_sq, y_sq = pack(x, y, lw, g)
    xz = jnp.stack([xp] + [lax.ppermute(xp, "tgt", hop(k)) for k in (1, 2, 3)])
    yh = jnp.stack([yp, lax.ppermute(yp, "src", swap(2))])
    xs = [xz] + [lax.ppermute(xz, "tgt", ring(k)) for k in (1, 2, 3)]
    yy = [yh] + [lax.ppermute(yh, "src", hop(k)) for k in (1, 2, 3)]
    ys = [jnp.concatenate([a, lax.ppermute(a, "src", swap(1))]) for a in yy]

    row = entries[:, 0] % SIDE
    col = entries[:, 1] // SIDE
    my_z, my_x = tgt_id // 4, tgt_id % 4
    my_y, my_h, my_c = src_id // 4, (src_id // 2) % 2, src_id % 2
    xat = ((my_x - row % 4) % 4) * 4 + (my_z - row // 4) % 4
    yat = ((my_y - col // 4) % 4) * 4 + (my_c ^ (col % 2)) * 2 + (my_h ^ ((col // 2) % 2))
    at = jnp.arange(SIDE, dtype=jnp.int32)
    where = ((my_z - at % 4) % 4) * 4 + (my_x - at // 4) % 4

    part, aux, tiles = row_pass(count, row, xat, yat, where, xs, ys)

    def all_sum(a, shift):
        far = [lax.ppermute(a, "tgt", shift(k)) for k in (1, 2, 3)]
        return (a + far[1]) + (far[0] + far[2])

    total = all_sum(all_sum(part, ring), hop)
    f_own, t_part = col_pass(
        count, row, col, tgt_id.reshape(1), total, aux, x_sq, tiles
    )
    t_all = lax.all_to_all(t_part, "src", 0, 0, tiled=True)
    return f_own.reshape(BLOCK), jnp.sum(t_all, axis=0), ln2 * aux[18] * epsilon + y_sq.reshape(BLOCK)


def on_device(
    source_points, target_points, source_logw, target_logw, potential_in, pair_list, pair_counts
):
    tgt_id = lax.axis_index("tgt")
    src_id = lax.axis_index("src")
    f_own, t_own, offset = fast_form(
        source_points, target_points, source_logw, potential_in, pair_list[0], pair_counts,
        tgt_id, src_id,
    )
    g_own = epsilon * target_logw - epsilon * jnp.log(t_own) + offset
    out_of_range = jnp.any(jnp.isnan(t_own))
    return lax.cond(
        out_of_range,
        plain_form,
        lambda *_: (f_own, g_own),
        source_points, target_points, source_logw, target_logw, potential_in, pair_list, pair_counts,
    )


def solution(mesh):
    return jax.shard_map(
        on_device,
        mesh=mesh,
        in_specs=(
            P(None, ("src", "tgt")),
            P(None, ("src", "tgt")),
            P(("src", "tgt")),
            P(("src", "tgt")),
            P(("src", "tgt")),
            P(("src", "tgt"), None, None),
            P(("src", "tgt")),
        ),
        out_specs=(P(("src", "tgt")), P(("src", "tgt"))),
        check_vma=False,
    )
```

```python
import functools

import jax
import jax.numpy as jnp
from jax import lax
from jax.experimental import pallas as pl
from jax.experimental.pallas import tpu as pltpu
from jax.sharding import PartitionSpec as P

epsilon = 0.25
lowest_log = -1e30
log2e = 1.4426950408889634
ln2 = 0.6931471805599453
SIDE = 16
BLOCK = 256
FEAT = 64
ROWS = 72
UNROLL = 8
vmem_bytes = 24 * 1024 * 1024
full_tiles = 128


def merge_pair(first, second):
    highest = jnp.maximum(first[0], second[0])
    summed = first[1] * jnp.exp(first[0] - highest) + second[1] * jnp.exp(second[0] - highest)
    return (highest, summed)


def cross_cost(left_all, left_sq, row_id, right_all, right_sq, col_id, block_len):
    left_points = lax.dynamic_slice_in_dim(left_all, row_id * block_len, block_len, 1)
    right_points = lax.dynamic_slice_in_dim(right_all, col_id * block_len, block_len, 1)
    left_norm = lax.dynamic_slice_in_dim(left_sq, row_id * block_len, block_len, 0)
    right_norm = lax.dynamic_slice_in_dim(right_sq, col_id * block_len, block_len, 0)
    inner_prod = lax.dot_general(
        left_points,
        right_points,
        (((0,), (0,)), ((), ())),
        precision=lax.Precision.HIGHEST,
        preferred_element_type=jnp.float32,
    )
    return left_norm[:, None] + right_norm[None, :] - 2.0 * inner_prod


def fold_part(running, position, highest, summed):
    old_high = lax.dynamic_slice_in_dim(running[0], position, 1, 0)[0]
    old_sum = lax.dynamic_slice_in_dim(running[1], position, 1, 0)[0]
    new_high, new_sum = merge_pair((old_high, old_sum), (highest, summed))
    return (
        lax.dynamic_update_slice_in_dim(running[0], new_high[None, :], position, 0),
        lax.dynamic_update_slice_in_dim(running[1], new_sum[None, :], position, 0),
    )


def gather_blocks(points, axis):
    copies = jnp.broadcast_to(points, (lax.axis_size(axis), *points.shape))
    blocks = lax.all_to_all(copies, axis, 0, 0, tiled=True)
    return jnp.moveaxis(blocks, 0, 1).reshape(points.shape[0], -1)


def plain_form(
    source_points, target_points, source_logw, target_logw, potential_in, pair_list, pair_counts
):
    n_tgt = lax.axis_size("tgt")
    n_src = lax.axis_size("src")
    block_len = source_points.shape[1]
    group_points = gather_blocks(source_points, "tgt")
    group_logw = lax.all_gather(source_logw, "tgt", axis=0, tiled=True)
    column_points = gather_blocks(target_points, "src")
    column_g = lax.all_gather(potential_in, "src", axis=0, tiled=True)
    group_sq = jnp.sum(group_points * group_points, axis=0)
    column_sq = jnp.sum(column_points * column_points, axis=0)
    row_start = (
        jnp.full((n_tgt, block_len), lowest_log, dtype=jnp.float32),
        jnp.zeros((n_tgt, block_len), dtype=jnp.float32),
    )
    col_start = (
        jnp.full((n_src, block_len), lowest_log, dtype=jnp.float32),
        jnp.zeros((n_src, block_len), dtype=jnp.float32),
    )
    own_entries = pair_list[0]
    own_count = pair_counts[0]

    def row_visit_pair(slot_id, carry):
        row_id = own_entries[slot_id, 0] % n_tgt
        col_id = own_entries[slot_id, 1] // n_tgt
        tile_cost = cross_cost(
            group_points, group_sq, row_id, column_points, column_sq, col_id, block_len
        )
        g_piece = lax.dynamic_slice_in_dim(column_g, col_id * block_len, block_len, 0)
        scores = (g_piece[None, :] - tile_cost) / epsilon
        highest = jnp.max(scores, axis=1)
        summed = jnp.sum(jnp.exp(scores - highest[:, None]), axis=1)
        return fold_part(carry, row_id, highest, summed)

    row_parts = lax.fori_loop(0, own_count, row_visit_pair, row_start)
    row_high = lax.pmax(row_parts[0], "tgt")
    row_sum = lax.psum(row_parts[1] * jnp.exp(row_parts[0] - row_high), "tgt")
    f_group = epsilon * group_logw - epsilon * (row_high + jnp.log(row_sum)).reshape(-1)
    f_own = lax.dynamic_slice_in_dim(f_group, lax.axis_index("tgt") * block_len, block_len, 0)

    def col_visit_pair(slot_id, carry):
        row_id = own_entries[slot_id, 0] % n_tgt
        col_id = own_entries[slot_id, 1] // n_tgt
        tile_cost = cross_cost(
            group_points, group_sq, row_id, column_points, column_sq, col_id, block_len
        )
        f_piece = lax.dynamic_slice_in_dim(f_group, row_id * block_len, block_len, 0)
        scores = (f_piece[:, None] - tile_cost) / epsilon
        highest = jnp.max(scores, axis=0)
        summed = jnp.sum(jnp.exp(scores - highest[None, :]), axis=0)
        return fold_part(carry, col_id, highest, summed)

    col_parts = lax.fori_loop(0, own_count, col_visit_pair, col_start)
    col_high = lax.pmax(col_parts[0], "src")
    col_sum = lax.psum(col_parts[1] * jnp.exp(col_parts[0] - col_high), "src")
    own_high = lax.dynamic_slice_in_dim(col_high, lax.axis_index("src"), 1, 0)[0]
    own_sum = lax.dynamic_slice_in_dim(col_sum, lax.axis_index("src"), 1, 0)[0]
    g_own = epsilon * target_logw - epsilon * (own_high + jnp.log(own_sum))
    return (f_own, g_own)


smem = pl.BlockSpec(memory_space=pltpu.SMEM)
vmem = pl.BlockSpec(memory_space=pltpu.VMEM)


def f32(*shape):
    return jax.ShapeDtypeStruct(shape, jnp.float32)


def pack_kernel(
    count_ref, ent_ref, x_ref, y_ref, lw_ref, g_ref, xp_ref, yp_ref, xsq_ref, ysq_ref, out_ref
):
    x = x_ref[...]
    y = y_ref[...]
    y_sq = jnp.sum(y * y, axis=0, keepdims=True)
    b = (4.0 * log2e) * (g_ref[...] - y_sq)
    row = lax.broadcasted_iota(jnp.int32, (8, BLOCK), 0)
    b_max = jnp.max(b, axis=1, keepdims=True)
    xp_ref[0:FEAT, :] = x
    xp_ref[FEAT:ROWS, :] = jnp.where(row == 0, lw_ref[...], b_max)
    yp_ref[0:FEAT, :] = y
    yp_ref[FEAT:ROWS, :] = jnp.broadcast_to(b, (8, BLOCK))
    xsq_ref[...] = jnp.sum(x * x, axis=0, keepdims=True)
    ysq_ref[...] = y_sq
    tgt_id, src_id, count = lax.axis_index("tgt"), lax.axis_index("src"), count_ref[0]
    my_z, my_x = tgt_id // 4, tgt_id % 4
    my_y, my_h, my_c = src_id // 4, (src_id // 2) % 2, src_id % 2
    lane = lax.broadcasted_iota(jnp.int32, (1, full_tiles), 1)
    live = lane < count

    def ordered(key, code):
        tall = jnp.broadcast_to(key, (full_tiles, full_tiles)).T
        rank = jnp.sum(jnp.where(tall < key, 1, 0), axis=0, keepdims=True)
        spot = jnp.broadcast_to(rank, (full_tiles, full_tiles)).T
        tall_code = jnp.broadcast_to(code, (full_tiles, full_tiles)).T
        return jnp.sum(jnp.where(spot == lane, tall_code, 0), axis=0, keepdims=True)

    def how_many(mask):
        return jnp.sum(jnp.where(mask, 1, 0), axis=1, keepdims=True)

    row = ent_ref[0:1, :] & 15
    col = ent_ref[1:2, :] >> 4
    q = (my_x - (row & 3)) & 3
    p = (my_z - (row >> 2)) & 3
    h = ((col >> 1) & 1) ^ my_h
    c = (col & 1) ^ my_c
    yat = ((my_y - (col >> 2)) & 3) * 4 + c * 2 + h
    dy = (col >> 2) ^ my_y
    spot = h * 8 + c * 4 + (dy ^ (dy >> 1))
    stage = jnp.where(q == 0, 0, jnp.where(q == 2, 2, 1))
    code = row + spot * 16 + (q * 4 + p) * 256 + yat * 4096
    code = ordered(jnp.where(live, stage, 3) * 128 + lane, jnp.where(live, code, 0))
    far = (code & 128) != 0
    code_b = (code & 127) + lane * 256
    code_b = ordered(jnp.where(live, jnp.where(far, 0, 1), 2) * 128 + lane, code_b)
    out_ref[0:1, :] = code
    out_ref[1:2, :] = code_b
    first = how_many(live & (stage == 0))
    second = how_many(live & (stage <= 1))
    away = how_many(live & far)
    out_ref[2:3, :] = jnp.where(lane == 0, first, jnp.where(lane == 1, second, jnp.where(lane == 2, away, count)))
    out_ref[3:8, :] = jnp.zeros((5, full_tiles), jnp.int32)


def pack(count, entries, x, y, lw, g):
    return pl.pallas_call(
        pack_kernel,
        out_shape=(
            f32(ROWS, BLOCK), f32(ROWS, BLOCK), f32(1, BLOCK), f32(1, BLOCK),
            jax.ShapeDtypeStruct((8, full_tiles), jnp.int32),
        ),
        in_specs=[smem] + [vmem] * 5,
        out_specs=[vmem] * 5,
        name="pack",
    )(count, entries.T, x, y, lw.reshape(1, BLOCK), g.reshape(1, BLOCK))


def prepare_source(x, at, xa):
    x = x * (8.0 * log2e)
    hi = x.astype(jnp.bfloat16)
    lo = (x - hi.astype(jnp.float32)).astype(jnp.bfloat16)
    xa[at, 0:64, :] = hi
    xa[at, 64:128, :] = lo
    xa[at, 128:192, :] = hi
    xa[at, 192:256, :] = lo


def note_source(block, q, p, aux_ref):
    tgt_id = lax.axis_index("tgt")
    where = ((tgt_id // 4 - p) & 3) * 4 + ((tgt_id % 4 - q) & 3)
    mean = jnp.sum(block[0:FEAT], axis=1, keepdims=True) * (1.0 / BLOCK)
    aux_ref[pl.ds(where, 1), :] = block[FEAT : FEAT + 1]
    aux_ref[16:17, :] = jnp.maximum(aux_ref[16:17, :], block[FEAT + 1 : FEAT + 2])
    aux_ref[17:18, :] = jnp.maximum(aux_ref[17:18, :], jnp.sum(mean * mean, axis=0, keepdims=True))


def visit_tiles(plan_ref, begin, end, slot_of, xa, ya, ub, k_ref, acc_ref):
    def group(step, carry):
        for u in range(UNROLL):
            raw = begin + step * UNROLL + u
            slot = jnp.minimum(raw, end - 1)
            code = plan_ref[0, slot]
            xat = slot_of((code >> 8) & 15)
            yat = (code >> 12) & 15
            row = code & 15
            scores = jnp.dot(ya[yat], xa[xat], preferred_element_type=jnp.float32)
            tile = jnp.exp2(scores)
            k_ref[slot] = tile.astype(jnp.bfloat16)
            weight = ub[yat]
            left = jnp.sum((tile[:, 0:128] * weight).reshape(32, 8, 128), axis=0)
            right = jnp.sum((tile[:, 128:256] * weight).reshape(32, 8, 128), axis=0)
            live = raw < end
            acc_ref[row, :, 0:128] += jnp.where(live, left, 0.0)
            acc_ref[row, :, 128:256] += jnp.where(live, right, 0.0)
        return carry

    lax.fori_loop(0, pl.cdiv(end - begin, UNROLL), group, 0)


def first_kernel(
    plan_ref, x0, y0, z0, y1, z1, y2, z2, y3, z3,
    ya, ub, k_ref, acc_ref, aux_ref, stat_ref, xa, codes, sem,
):
    fetch = pltpu.make_async_copy(plan_ref, codes, sem)
    fetch.start()
    ys = (y0, z0, y1, z1, y2, z2, y3, z3)
    lines = [ys[at // 2][at % 2, FEAT : FEAT + 1, :] for at in range(SIDE)]
    top = jnp.max(functools.reduce(jnp.maximum, lines), axis=1, keepdims=True)
    low = jnp.min(functools.reduce(jnp.minimum, lines), axis=1, keepdims=True) - top
    y_sq = jnp.zeros((1, BLOCK), jnp.float32)
    for at in range(SIDE):
        y = ys[at // 2][at % 2, 0:FEAT, :]
        y_sq = jnp.maximum(y_sq, jnp.sum(y * y, axis=0, keepdims=True))
        turned = jnp.concatenate([y, y], axis=0).T
        hi = turned.astype(jnp.bfloat16)
        lo = (turned - hi.astype(jnp.float32)).astype(jnp.bfloat16)
        ya[at, :, 0:128] = hi
        ya[at, :, 128:256] = lo
        ub[at] = jnp.exp2(jnp.broadcast_to(lines[at] - top, (128, BLOCK)).T)
    stat_ref[0:1, :] = jnp.broadcast_to(low, (1, BLOCK))
    stat_ref[1:2, :] = jnp.broadcast_to(top, (1, BLOCK))
    stat_ref[2:3, :] = y_sq
    stat_ref[3:8, :] = jnp.zeros((5, BLOCK), jnp.float32)
    aux_ref[0:16, :] = jnp.zeros((16, BLOCK), jnp.float32)
    aux_ref[16:17, :] = jnp.full((1, BLOCK), -1e30, jnp.float32)
    aux_ref[17:24, :] = jnp.zeros((7, BLOCK), jnp.float32)
    for p in range(4):
        block = x0[p]
        prepare_source(block[0:FEAT], p, xa)
        note_source(block, 0, p, aux_ref)
    acc_ref[...] = jnp.zeros_like(acc_ref)
    fetch.wait()
    visit_tiles(codes, 0, codes[2, 0], lambda at: at, xa, ya, ub, k_ref, acc_ref)


def second_kernel(
    plan_ref, x1, x3, ya, ub, k_in, acc_in, aux_in, k_ref, acc_ref, aux_ref, xa, codes, sem
):
    fetch = pltpu.make_async_copy(plan_ref, codes, sem)
    fetch.start()
    aux_ref[...] = aux_in[...]
    acc_ref[...] = acc_in[...]
    for q, x_ref, base in ((1, x1, 0), (3, x3, 4)):
        for p in range(4):
            block = x_ref[p]
            prepare_source(block[0:FEAT], base + p, xa)
            note_source(block, q, p, aux_ref)
    fetch.wait()
    visit_tiles(
        codes, codes[2, 0], codes[2, 1],
        lambda at: (at & 3) + ((at >> 3) & 1) * 4, xa, ya, ub, k_ref, acc_ref,
    )


def third_kernel(
    plan_ref, xl, xr, ya, ub, k_in, acc_in, aux_in, stat_ref, k_ref, s_ref, aux_ref, xa, acc, codes, sem
):
    fetch = pltpu.make_async_copy(plan_ref, codes, sem)
    fetch.start()
    aux_ref[...] = aux_in[...]
    acc[...] = acc_in[...]
    for p in range(4):
        block = xl[p] if p < 2 else xr[p - 2]
        prepare_source(block[0:FEAT], p, xa)
        note_source(block, 2, p, aux_ref)
    fetch.wait()
    visit_tiles(codes, codes[2, 1], codes[2, 3], lambda at: at & 3, xa, ya, ub, k_ref, acc)
    total = jnp.sum(acc[...], axis=1)
    low = stat_ref[0:1, 0:1]
    top = stat_ref[1:2, 0:1]
    shift = aux_ref[16:17, 0:1]
    lean = (8.0 * log2e) * jnp.sqrt(aux_ref[17:18, 0:1] * jnp.max(stat_ref[2:3, :], axis=1, keepdims=True))
    most = jnp.max(jnp.max(total, axis=0, keepdims=True), axis=1, keepdims=True)
    apart = top - shift
    good = (
        (lean <= 24.0)
        & (low >= -105.0)
        & (jnp.abs(apart) <= 16.0)
        & (most <= jnp.exp2(120.0 + low))
    )
    s_ref[...] = jnp.where(good, total * jnp.exp2(apart), jnp.nan)
    aux_ref[18:19, :] = jnp.broadcast_to(apart, (1, BLOCK))


tiles_shape = pltpu.VMEM((full_tiles, BLOCK, BLOCK), jnp.bfloat16)
target_shape = pltpu.VMEM((SIDE, BLOCK, BLOCK), jnp.bfloat16)
weight_shape = pltpu.VMEM((SIDE, BLOCK, 128), jnp.float32)
row_cost = dict(flops=32 * 2 * BLOCK**3, bytes_accessed=1 << 20, transcendentals=32 * BLOCK * BLOCK)


codes_scratch = [pltpu.SMEM((8, full_tiles), jnp.int32), pltpu.SemaphoreType.DMA]


def source_scratch(blocks):
    return pltpu.VMEM((blocks, BLOCK, BLOCK), jnp.bfloat16)


def first_pass(order, x0, ys):
    return pl.pallas_call(
        first_kernel,
        out_shape=(
            target_shape, weight_shape, tiles_shape,
            f32(SIDE, 8, BLOCK), f32(24, BLOCK), f32(8, BLOCK),
        ),
        in_specs=[vmem] * 10,
        out_specs=[vmem] * 6,
        scratch_shapes=[source_scratch(4), *codes_scratch],
        compiler_params=pltpu.CompilerParams(vmem_limit_bytes=vmem_bytes),
        cost_estimate=pl.CostEstimate(**row_cost),
        name="row_pass_a",
    )(order, x0, *ys)


def second_pass(order, x1, x3, ya, ub, tiles, acc, aux):
    return pl.pallas_call(
        second_kernel,
        out_shape=(tiles_shape, f32(SIDE, 8, BLOCK), f32(24, BLOCK)),
        in_specs=[vmem] * 8,
        out_specs=[vmem] * 3,
        scratch_shapes=[source_scratch(8), *codes_scratch],
        input_output_aliases={5: 0},
        compiler_params=pltpu.CompilerParams(vmem_limit_bytes=vmem_bytes),
        cost_estimate=pl.CostEstimate(**row_cost),
        name="row_pass_b",
    )(order, x1, x3, ya, ub, tiles, acc, aux)


def third_pass(order, xl, xr, ya, ub, tiles, acc, aux, stat):
    return pl.pallas_call(
        third_kernel,
        out_shape=(tiles_shape, f32(SIDE, BLOCK), f32(24, BLOCK)),
        in_specs=[vmem] * 9,
        out_specs=[vmem] * 3,
        scratch_shapes=[source_scratch(4), pltpu.VMEM((SIDE, 8, BLOCK), jnp.float32), *codes_scratch],
        input_output_aliases={5: 0},
        compiler_params=pltpu.CompilerParams(vmem_limit_bytes=vmem_bytes),
        cost_estimate=pl.CostEstimate(**row_cost),
        name="row_pass_c",
    )(order, xl, xr, ya, ub, tiles, acc, aux, stat)


def visit_columns(plan_ref, begin, end, v_ref, k_ref, t_ref, acc):
    acc[...] = jnp.zeros_like(acc)

    def group(step, carry):
        for u in range(UNROLL):
            raw = begin + step * UNROLL + u
            code = plan_ref[1, jnp.minimum(raw, end - 1)]
            v = jnp.where(raw < end, v_ref[pl.ds(code & 15, 1), :], 0.0)
            tile = k_ref[code >> 8].astype(jnp.float32)
            acc[(code >> 4) & 7] += tile[:, 0:128] * v[:, 0:128] + tile[:, 128:256] * v[:, 128:256]
        return carry

    lax.fori_loop(0, pl.cdiv(end - begin, UNROLL), group, 0)
    ones = jnp.ones((16, 128), jnp.bfloat16)
    across = (((1,), (1,)), ((), ()))
    for c in range(8):
        rest = acc[c]
        total = jnp.zeros((16, BLOCK), jnp.float32)
        for _ in range(3):
            part = rest.astype(jnp.bfloat16)
            rest = rest - part.astype(jnp.float32)
            total += lax.dot_general(ones, part, across, preferred_element_type=jnp.float32)
        t_ref[c : c + 1, :] = total[0:1, :]


def far_kernel(plan_ref, s_ref, aux_ref, xsq_ref, k_ref, f_ref, v_ref, t_ref, acc, codes, sem):
    fetch = pltpu.make_async_copy(plan_ref, codes, sem)
    fetch.start()
    total = s_ref[...]
    v = jnp.exp(aux_ref[0:16, :]) / total * jnp.exp2(aux_ref[18:19, :])
    fine = jnp.where((total >= 1.5e-11) & (total <= 4.3e12), 1.0, 0.0)
    fine = jnp.min(jnp.min(fine, axis=1, keepdims=True), axis=0, keepdims=True) > 0.5
    v_ref[...] = jnp.where(fine, v, jnp.nan)
    own = lax.axis_index("tgt")
    own_s = s_ref[pl.ds(own, 1), :]
    own_lw = aux_ref[pl.ds(own, 1), :]
    f_ref[...] = epsilon * own_lw - epsilon * (jnp.log(own_s) + ln2 * aux_ref[16:17, :]) + xsq_ref[...]
    fetch.wait()
    visit_columns(codes, 0, codes[2, 2], v_ref, k_ref, t_ref, acc)
    t_ref[...] += jnp.where(fine, 0.0, jnp.nan)


def near_kernel(plan_ref, v_ref, k_ref, t_ref, acc, codes, sem):
    fetch = pltpu.make_async_copy(plan_ref, codes, sem)
    fetch.start()
    fetch.wait()
    visit_columns(codes, codes[2, 2], codes[2, 3], v_ref, k_ref, t_ref, acc)


def far_pass(order, total, aux, xsq, tiles):
    return pl.pallas_call(
        far_kernel,
        out_shape=(f32(1, BLOCK), f32(SIDE, BLOCK), f32(8, BLOCK)),
        in_specs=[vmem] * 5,
        out_specs=[vmem] * 3,
        scratch_shapes=[pltpu.VMEM((8, BLOCK, 128), jnp.float32), *codes_scratch],
        compiler_params=pltpu.CompilerParams(vmem_limit_bytes=vmem_bytes),
        cost_estimate=pl.CostEstimate(**row_cost),
        name="col_pass_a",
    )(order, total, aux, xsq, tiles)


def near_pass(order, v, tiles):
    return pl.pallas_call(
        near_kernel,
        out_shape=f32(8, BLOCK),
        in_specs=[vmem] * 3,
        out_specs=vmem,
        scratch_shapes=[pltpu.VMEM((8, BLOCK, 128), jnp.float32), *codes_scratch],
        compiler_params=pltpu.CompilerParams(vmem_limit_bytes=vmem_bytes),
        cost_estimate=pl.CostEstimate(**row_cost),
        name="col_pass_b",
    )(order, v, tiles)


def ring(k):
    return [(i, (i // 4) * 4 + (i + k) % 4) for i in range(SIDE)]


def hop(k):
    return [(i, (i + 4 * k) % SIDE) for i in range(SIDE)]


def swap(bits):
    return [(i, i ^ bits) for i in range(SIDE)]


def fast_form(x, y, lw, g, entries, count):
    xp, yp, x_sq, y_sq, order = pack(count, entries, x, y, lw, g)
    xz = jnp.stack([xp] + [lax.ppermute(xp, "tgt", hop(k)) for k in (1, 2, 3)])
    yh = jnp.stack([yp, lax.ppermute(yp, "src", swap(2))])
    x1 = lax.ppermute(xz, "tgt", ring(1))
    x3 = lax.ppermute(xz, "tgt", ring(3))
    yy = [yh] + [lax.ppermute(yh, "src", hop(k)) for k in (1, 2, 3)]
    xl = lax.ppermute(x1[0:2], "tgt", ring(1))
    xr = lax.ppermute(x3[2:4], "tgt", ring(3))
    ys = [z for a in yy for z in (a, lax.ppermute(a, "src", swap(1)))]

    ya, ub, tiles, acc, aux, stat = first_pass(order, xz, ys)
    tiles, acc, aux = second_pass(order, x1, x3, ya, ub, tiles, acc, aux)
    tiles, total, aux = third_pass(order, xl, xr, ya, ub, tiles, acc, aux, stat)

    def all_sum(a, shift):
        far = [lax.ppermute(a, "tgt", shift(k)) for k in (1, 2, 3)]
        return (a + far[1]) + (far[0] + far[2])

    total = all_sum(all_sum(total, ring), hop)

    f_own, v, away = far_pass(order, total, aux, x_sq, tiles)
    from_far = lax.ppermute(away, "src", swap(2))
    part = near_pass(order, v, tiles) + from_far
    part = part[0:4] + lax.ppermute(part[4:8], "src", swap(1))
    part = (
        part[0:1]
        + lax.ppermute(part[1:2], "src", swap(4))
        + lax.ppermute(part[2:3], "src", swap(12))
        + lax.ppermute(part[3:4], "src", swap(8))
    )
    offset = epsilon * ln2 * stat[1] + y_sq.reshape(BLOCK)
    return f_own.reshape(BLOCK), part.reshape(BLOCK), offset


def on_device(
    source_points, target_points, source_logw, target_logw, potential_in, pair_list, pair_counts
):
    f_own, t_own, offset = fast_form(
        source_points, target_points, source_logw, potential_in, pair_list[0], pair_counts
    )
    g_own = epsilon * target_logw - epsilon * jnp.log(t_own) + offset
    out_of_range = jnp.isnan(t_own[0])
    return lax.cond(
        out_of_range,
        plain_form,
        lambda *_: (f_own, g_own),
        source_points, target_points, source_logw, target_logw, potential_in, pair_list, pair_counts,
    )


def solution(mesh):
    return jax.shard_map(
        on_device,
        mesh=mesh,
        in_specs=(
            P(None, ("src", "tgt")),
            P(None, ("src", "tgt")),
            P(("src", "tgt")),
            P(("src", "tgt")),
            P(("src", "tgt")),
            P(("src", "tgt"), None, None),
            P(("src", "tgt")),
        ),
        out_specs=(P(("src", "tgt")), P(("src", "tgt"))),
        check_vma=False,
    )
```

```python
import functools

import jax
import jax.numpy as jnp
from jax import lax
from jax.experimental import pallas as pl
from jax.experimental.pallas import tpu as pltpu
from jax.sharding import PartitionSpec as P

epsilon = 0.25
lowest_log = -1e30
log2e = 1.4426950408889634
ln2 = 0.6931471805599453
SIDE = 16
BLOCK = 256
FEAT = 64
ROWS = 72
UNROLL = 8
vmem_bytes = 24 * 1024 * 1024
full_tiles = 128


def merge_pair(first, second):
    highest = jnp.maximum(first[0], second[0])
    summed = first[1] * jnp.exp(first[0] - highest) + second[1] * jnp.exp(second[0] - highest)
    return (highest, summed)


def cross_cost(left_all, left_sq, row_id, right_all, right_sq, col_id, block_len):
    left_points = lax.dynamic_slice_in_dim(left_all, row_id * block_len, block_len, 1)
    right_points = lax.dynamic_slice_in_dim(right_all, col_id * block_len, block_len, 1)
    left_norm = lax.dynamic_slice_in_dim(left_sq, row_id * block_len, block_len, 0)
    right_norm = lax.dynamic_slice_in_dim(right_sq, col_id * block_len, block_len, 0)
    inner_prod = lax.dot_general(
        left_points,
        right_points,
        (((0,), (0,)), ((), ())),
        precision=lax.Precision.HIGHEST,
        preferred_element_type=jnp.float32,
    )
    return left_norm[:, None] + right_norm[None, :] - 2.0 * inner_prod


def fold_part(running, position, highest, summed):
    old_high = lax.dynamic_slice_in_dim(running[0], position, 1, 0)[0]
    old_sum = lax.dynamic_slice_in_dim(running[1], position, 1, 0)[0]
    new_high, new_sum = merge_pair((old_high, old_sum), (highest, summed))
    return (
        lax.dynamic_update_slice_in_dim(running[0], new_high[None, :], position, 0),
        lax.dynamic_update_slice_in_dim(running[1], new_sum[None, :], position, 0),
    )


def gather_blocks(points, axis):
    copies = jnp.broadcast_to(points, (lax.axis_size(axis), *points.shape))
    blocks = lax.all_to_all(copies, axis, 0, 0, tiled=True)
    return jnp.moveaxis(blocks, 0, 1).reshape(points.shape[0], -1)


def plain_form(
    source_points, target_points, source_logw, target_logw, potential_in, pair_list, pair_counts
):
    n_tgt = lax.axis_size("tgt")
    n_src = lax.axis_size("src")
    block_len = source_points.shape[1]
    group_points = gather_blocks(source_points, "tgt")
    group_logw = lax.all_gather(source_logw, "tgt", axis=0, tiled=True)
    column_points = gather_blocks(target_points, "src")
    column_g = lax.all_gather(potential_in, "src", axis=0, tiled=True)
    group_sq = jnp.sum(group_points * group_points, axis=0)
    column_sq = jnp.sum(column_points * column_points, axis=0)
    row_start = (
        jnp.full((n_tgt, block_len), lowest_log, dtype=jnp.float32),
        jnp.zeros((n_tgt, block_len), dtype=jnp.float32),
    )
    col_start = (
        jnp.full((n_src, block_len), lowest_log, dtype=jnp.float32),
        jnp.zeros((n_src, block_len), dtype=jnp.float32),
    )
    own_entries = pair_list[0]
    own_count = pair_counts[0]

    def row_visit_pair(slot_id, carry):
        row_id = own_entries[slot_id, 0] % n_tgt
        col_id = own_entries[slot_id, 1] // n_tgt
        tile_cost = cross_cost(
            group_points, group_sq, row_id, column_points, column_sq, col_id, block_len
        )
        g_piece = lax.dynamic_slice_in_dim(column_g, col_id * block_len, block_len, 0)
        scores = (g_piece[None, :] - tile_cost) / epsilon
        highest = jnp.max(scores, axis=1)
        summed = jnp.sum(jnp.exp(scores - highest[:, None]), axis=1)
        return fold_part(carry, row_id, highest, summed)

    row_parts = lax.fori_loop(0, own_count, row_visit_pair, row_start)
    row_high = lax.pmax(row_parts[0], "tgt")
    row_sum = lax.psum(row_parts[1] * jnp.exp(row_parts[0] - row_high), "tgt")
    f_group = epsilon * group_logw - epsilon * (row_high + jnp.log(row_sum)).reshape(-1)
    f_own = lax.dynamic_slice_in_dim(f_group, lax.axis_index("tgt") * block_len, block_len, 0)

    def col_visit_pair(slot_id, carry):
        row_id = own_entries[slot_id, 0] % n_tgt
        col_id = own_entries[slot_id, 1] // n_tgt
        tile_cost = cross_cost(
            group_points, group_sq, row_id, column_points, column_sq, col_id, block_len
        )
        f_piece = lax.dynamic_slice_in_dim(f_group, row_id * block_len, block_len, 0)
        scores = (f_piece[:, None] - tile_cost) / epsilon
        highest = jnp.max(scores, axis=0)
        summed = jnp.sum(jnp.exp(scores - highest[None, :]), axis=0)
        return fold_part(carry, col_id, highest, summed)

    col_parts = lax.fori_loop(0, own_count, col_visit_pair, col_start)
    col_high = lax.pmax(col_parts[0], "src")
    col_sum = lax.psum(col_parts[1] * jnp.exp(col_parts[0] - col_high), "src")
    own_high = lax.dynamic_slice_in_dim(col_high, lax.axis_index("src"), 1, 0)[0]
    own_sum = lax.dynamic_slice_in_dim(col_sum, lax.axis_index("src"), 1, 0)[0]
    g_own = epsilon * target_logw - epsilon * (own_high + jnp.log(own_sum))
    return (f_own, g_own)


smem = pl.BlockSpec(memory_space=pltpu.SMEM)
vmem = pl.BlockSpec(memory_space=pltpu.VMEM)


def f32(*shape):
    return jax.ShapeDtypeStruct(shape, jnp.float32)


def pack_kernel(
    count_ref, ent_ref, x_ref, y_ref, lw_ref, g_ref, xp_ref, yp_ref, xsq_ref, ysq_ref, out_ref
):
    x = x_ref[...]
    y = y_ref[...]
    y_sq = jnp.sum(y * y, axis=0, keepdims=True)
    b = (4.0 * log2e) * (g_ref[...] - y_sq)
    row = lax.broadcasted_iota(jnp.int32, (8, BLOCK), 0)
    b_max = jnp.max(b, axis=1, keepdims=True)
    xp_ref[0:FEAT, :] = x
    xp_ref[FEAT:ROWS, :] = jnp.where(row == 0, lw_ref[...], b_max)
    yp_ref[0:FEAT, :] = y
    yp_ref[FEAT:ROWS, :] = jnp.broadcast_to(b, (8, BLOCK))
    xsq_ref[...] = jnp.sum(x * x, axis=0, keepdims=True)
    ysq_ref[...] = y_sq
    tgt_id, src_id, count = lax.axis_index("tgt"), lax.axis_index("src"), count_ref[0]
    my_z, my_x = tgt_id // 4, tgt_id % 4
    my_y, my_h, my_c = src_id // 4, (src_id // 2) % 2, src_id % 2
    lane = lax.broadcasted_iota(jnp.int32, (1, full_tiles), 1)
    live = lane < count

    def ordered(key, code):
        tall = jnp.broadcast_to(key, (full_tiles, full_tiles)).T
        rank = jnp.sum(jnp.where(tall < key, 1, 0), axis=0, keepdims=True)
        spot = jnp.broadcast_to(rank, (full_tiles, full_tiles)).T
        tall_code = jnp.broadcast_to(code, (full_tiles, full_tiles)).T
        return jnp.sum(jnp.where(spot == lane, tall_code, 0), axis=0, keepdims=True)

    def how_many(mask):
        return jnp.sum(jnp.where(mask, 1, 0), axis=1, keepdims=True)

    row = ent_ref[0:1, :] & 15
    col = ent_ref[1:2, :] >> 4
    q = (my_x - (row & 3)) & 3
    p = my_z ^ (row >> 2)
    h = ((col >> 1) & 1) ^ my_h
    c = (col & 1) ^ my_c
    turn = (my_y - (col >> 2)) & 3
    yat = (turn ^ (turn >> 1)) * 4 + c * 2 + h
    dy = (col >> 2) ^ my_y
    spot = h * 8 + c * 4 + (dy ^ (dy >> 1))
    stage = jnp.where(q == 2, 1, 0)
    code = row + spot * 16 + (q * 4 + p) * 256 + yat * 4096
    code = ordered(jnp.where(live, stage, 3) * 128 + lane, jnp.where(live, code, 0))
    far = (code & 128) != 0
    code_b = (code & 127) + lane * 256
    code_b = ordered(jnp.where(live, jnp.where(far, 0, 1), 2) * 128 + lane, code_b)
    out_ref[0:1, :] = code
    out_ref[1:2, :] = code_b
    first = how_many(live & (stage == 0))
    away = how_many(live & far)
    out_ref[2:3, :] = jnp.where(lane == 0, first, jnp.where(lane == 2, away, count))
    out_ref[3:8, :] = jnp.zeros((5, full_tiles), jnp.int32)


def pack(count, entries, x, y, lw, g):
    return pl.pallas_call(
        pack_kernel,
        out_shape=(
            f32(ROWS, BLOCK), f32(ROWS, BLOCK),
            pltpu.VMEM((1, BLOCK), jnp.float32), pltpu.VMEM((1, BLOCK), jnp.float32),
            pltpu.VMEM((8, full_tiles), jnp.int32),
        ),
        in_specs=[smem] + [vmem] * 5,
        out_specs=[vmem] * 5,
        name="pack",
    )(count, entries.T, x, y, lw.reshape(1, BLOCK), g.reshape(1, BLOCK))


def prepare_source(x, at, xa):
    x = x * (8.0 * log2e)
    hi = x.astype(jnp.bfloat16)
    lo = (x - hi.astype(jnp.float32)).astype(jnp.bfloat16)
    xa[at, 0:64, :] = hi
    xa[at, 64:128, :] = lo
    xa[at, 128:192, :] = hi
    xa[at, 192:256, :] = lo


def note_source(block, q, p, aux_ref):
    tgt_id = lax.axis_index("tgt")
    where = ((tgt_id // 4) ^ p) * 4 + ((tgt_id % 4 - q) & 3)
    mean = jnp.sum(block[0:FEAT], axis=1, keepdims=True) * (1.0 / BLOCK)
    aux_ref[pl.ds(where, 1), :] = block[FEAT : FEAT + 1]
    aux_ref[16:17, :] = jnp.maximum(aux_ref[16:17, :], block[FEAT + 1 : FEAT + 2])
    aux_ref[17:18, :] = jnp.maximum(aux_ref[17:18, :], jnp.sum(mean * mean, axis=0, keepdims=True))


def visit_tiles(unroll, plan_ref, begin, end, xa, ya, ub, k_ref, acc_ref):
    def group(step, carry):
        for u in range(unroll):
            raw = begin + step * unroll + u
            slot = jnp.minimum(raw, end - 1)
            code = plan_ref[0, slot]
            xat = (code >> 8) & 15
            yat = (code >> 12) & 15
            row = code & 15
            scores = jnp.dot(ya[yat], xa[xat], preferred_element_type=jnp.float32)
            tile = jnp.exp2(scores)
            k_ref[slot] = tile.astype(jnp.bfloat16)
            weight = ub[yat]
            left = jnp.sum((tile[:, 0:128] * weight).reshape(32, 8, 128), axis=0)
            right = jnp.sum((tile[:, 128:256] * weight).reshape(32, 8, 128), axis=0)
            live = raw < end
            acc_ref[row, :, 0:128] += jnp.where(live, left, 0.0)
            acc_ref[row, :, 128:256] += jnp.where(live, right, 0.0)
        return carry

    lax.fori_loop(0, pl.cdiv(end - begin, unroll), group, 0)


def first_kernel(
    plan_ref, x0, x1, x3, y0, z0, y1, z1, y2, z2, y3, z3,
    ya, ub, k_ref, acc_ref, aux_ref, stat_ref, xa, codes, sem,
):
    fetch = pltpu.make_async_copy(plan_ref, codes, sem)
    fetch.start()
    ys = (y0, z0, y1, z1, y2, z2, y3, z3)
    lines = [ys[at // 2][at % 2, FEAT : FEAT + 1, :] for at in range(SIDE)]
    top = jnp.max(functools.reduce(jnp.maximum, lines), axis=1, keepdims=True)
    low = jnp.min(functools.reduce(jnp.minimum, lines), axis=1, keepdims=True) - top
    y_sq = jnp.zeros((1, BLOCK), jnp.float32)
    for at in range(SIDE):
        y = ys[at // 2][at % 2, 0:FEAT, :]
        y_sq = jnp.maximum(y_sq, jnp.sum(y * y, axis=0, keepdims=True))
        turned = jnp.concatenate([y, y], axis=0).T
        hi = turned.astype(jnp.bfloat16)
        lo = (turned - hi.astype(jnp.float32)).astype(jnp.bfloat16)
        ya[at, :, 0:128] = hi
        ya[at, :, 128:256] = lo
        ub[at] = jnp.broadcast_to(jnp.exp2(lines[at] - top), (128, BLOCK)).T
    stat_ref[0:1, :] = jnp.broadcast_to(low, (1, BLOCK))
    stat_ref[1:2, :] = jnp.broadcast_to(top, (1, BLOCK))
    stat_ref[2:3, :] = y_sq
    stat_ref[3:8, :] = jnp.zeros((5, BLOCK), jnp.float32)
    aux_ref[0:16, :] = jnp.zeros((16, BLOCK), jnp.float32)
    aux_ref[16:17, :] = jnp.full((1, BLOCK), -1e30, jnp.float32)
    aux_ref[17:24, :] = jnp.zeros((7, BLOCK), jnp.float32)
    for q, ref in ((0, x0), (1, x1), (3, x3)):
        for p in range(4):
            block = ref[p]
            prepare_source(block[0:FEAT], q * 4 + p, xa)
            note_source(block, q, p, aux_ref)
    acc_ref[...] = jnp.zeros_like(acc_ref)
    fetch.wait()
    visit_tiles(2 * UNROLL, codes, 0, codes[2, 0], xa, ya, ub, k_ref, acc_ref)


def second_kernel(
    plan_ref, x2, ya, ub, k_in, acc_in, aux_in, stat_ref,
    k_ref, s_ref, aux_ref, xa, acc, codes, sem,
):
    fetch = pltpu.make_async_copy(plan_ref, codes, sem)
    fetch.start()
    aux_ref[...] = aux_in[...]
    acc[...] = acc_in[...]
    for p in range(4):
        block = x2[p]
        prepare_source(block[0:FEAT], 8 + p, xa)
        note_source(block, 2, p, aux_ref)
    fetch.wait()
    visit_tiles(UNROLL, codes, codes[2, 0], codes[2, 3], xa, ya, ub, k_ref, acc)
    total = jnp.sum(acc[...], axis=1)
    low = stat_ref[0:1, 0:1]
    top = stat_ref[1:2, 0:1]
    shift = aux_ref[16:17, 0:1]
    lean = (8.0 * log2e) * jnp.sqrt(aux_ref[17:18, 0:1] * jnp.max(stat_ref[2:3, :], axis=1, keepdims=True))
    most = jnp.max(jnp.max(total, axis=0, keepdims=True), axis=1, keepdims=True)
    apart = top - shift
    good = (
        (lean <= 24.0)
        & (low >= -105.0)
        & (jnp.abs(apart) <= 16.0)
        & (most <= jnp.exp2(120.0 + low))
    )
    s_ref[...] = jnp.where(good, total * jnp.exp2(apart), jnp.nan)
    aux_ref[18:19, :] = jnp.broadcast_to(apart, (1, BLOCK))


tiles_shape = pltpu.VMEM((full_tiles, BLOCK, BLOCK), jnp.bfloat16)
target_shape = pltpu.VMEM((SIDE, BLOCK, BLOCK), jnp.bfloat16)
weight_shape = pltpu.VMEM((SIDE, BLOCK, 128), jnp.float32)
row_cost = dict(flops=32 * 2 * BLOCK**3, bytes_accessed=1 << 20, transcendentals=32 * BLOCK * BLOCK)


codes_scratch = [pltpu.SMEM((8, full_tiles), jnp.int32), pltpu.SemaphoreType.DMA]


def source_scratch(blocks):
    return pltpu.VMEM((blocks, BLOCK, BLOCK), jnp.bfloat16)


def first_pass(order, xs, ys):
    return pl.pallas_call(
        first_kernel,
        out_shape=(
            target_shape, weight_shape, tiles_shape,
            f32(SIDE, 8, BLOCK), f32(24, BLOCK), f32(8, BLOCK),
        ),
        in_specs=[vmem] * 12,
        out_specs=[vmem] * 6,
        scratch_shapes=[source_scratch(SIDE), *codes_scratch],
        compiler_params=pltpu.CompilerParams(vmem_limit_bytes=vmem_bytes),
        cost_estimate=pl.CostEstimate(**row_cost),
        name="row_pass_a",
    )(order, *xs, *ys)


def second_pass(order, x2, ya, ub, tiles, acc, aux, stat):
    return pl.pallas_call(
        second_kernel,
        out_shape=(tiles_shape, f32(SIDE, BLOCK), f32(24, BLOCK)),
        in_specs=[vmem] * 8,
        out_specs=[vmem] * 3,
        scratch_shapes=[source_scratch(SIDE), pltpu.VMEM((SIDE, 8, BLOCK), jnp.float32), *codes_scratch],
        input_output_aliases={4: 0},
        compiler_params=pltpu.CompilerParams(vmem_limit_bytes=vmem_bytes),
        cost_estimate=pl.CostEstimate(**row_cost),
        name="row_pass_b",
    )(order, x2, ya, ub, tiles, acc, aux, stat)


def visit_columns(plan_ref, begin, end, v_ref, k_ref, t_ref, acc):
    acc[...] = jnp.zeros_like(acc)

    def group(step, carry):
        for u in range(UNROLL):
            raw = begin + step * UNROLL + u
            code = plan_ref[1, jnp.minimum(raw, end - 1)]
            v = jnp.where(raw < end, v_ref[pl.ds(code & 15, 1), :], 0.0)
            tile = k_ref[code >> 8].astype(jnp.float32)
            acc[(code >> 4) & 7] += tile[:, 0:128] * v[:, 0:128] + tile[:, 128:256] * v[:, 128:256]
        return carry

    lax.fori_loop(0, pl.cdiv(end - begin, UNROLL), group, 0)
    ones = jnp.ones((16, 128), jnp.bfloat16)
    across = (((1,), (1,)), ((), ()))
    for c in range(8):
        rest = acc[c]
        total = jnp.zeros((16, BLOCK), jnp.float32)
        for _ in range(3):
            part = rest.astype(jnp.bfloat16)
            rest = rest - part.astype(jnp.float32)
            total += lax.dot_general(ones, part, across, preferred_element_type=jnp.float32)
        t_ref[c : c + 1, :] = total[0:1, :]


def far_kernel(plan_ref, s_ref, aux_ref, xsq_ref, k_ref, f_ref, v_ref, t_ref, acc, codes, sem):
    fetch = pltpu.make_async_copy(plan_ref, codes, sem)
    fetch.start()
    total = s_ref[...]
    v = jnp.exp(aux_ref[0:16, :]) / total * jnp.exp2(aux_ref[18:19, :])
    fine = jnp.where((total >= 1.5e-11) & (total <= 4.3e12), 1.0, 0.0)
    fine = jnp.min(jnp.min(fine, axis=1, keepdims=True), axis=0, keepdims=True) > 0.5
    v_ref[...] = jnp.where(fine, v, jnp.nan)
    own = lax.axis_index("tgt")
    own_s = s_ref[pl.ds(own, 1), :]
    own_lw = aux_ref[pl.ds(own, 1), :]
    f_ref[...] = epsilon * own_lw - epsilon * (jnp.log(own_s) + ln2 * aux_ref[16:17, :]) + xsq_ref[...]
    fetch.wait()
    visit_columns(codes, 0, codes[2, 2], v_ref, k_ref, t_ref, acc)
    t_ref[...] += jnp.where(fine, 0.0, jnp.nan)


def near_kernel(plan_ref, v_ref, k_ref, t_ref, acc, codes, sem):
    fetch = pltpu.make_async_copy(plan_ref, codes, sem)
    fetch.start()
    fetch.wait()
    visit_columns(codes, codes[2, 2], codes[2, 3], v_ref, k_ref, t_ref, acc)


def far_pass(order, total, aux, xsq, tiles):
    return pl.pallas_call(
        far_kernel,
        out_shape=(f32(1, BLOCK), f32(SIDE, BLOCK), f32(8, BLOCK)),
        in_specs=[vmem] * 5,
        out_specs=[vmem] * 3,
        scratch_shapes=[pltpu.VMEM((8, BLOCK, 128), jnp.float32), *codes_scratch],
        compiler_params=pltpu.CompilerParams(vmem_limit_bytes=vmem_bytes),
        cost_estimate=pl.CostEstimate(**row_cost),
        name="col_pass_a",
    )(order, total, aux, xsq, tiles)


def near_pass(order, v, tiles):
    return pl.pallas_call(
        near_kernel,
        out_shape=f32(8, BLOCK),
        in_specs=[vmem] * 3,
        out_specs=vmem,
        scratch_shapes=[pltpu.VMEM((8, BLOCK, 128), jnp.float32), *codes_scratch],
        compiler_params=pltpu.CompilerParams(vmem_limit_bytes=vmem_bytes),
        cost_estimate=pl.CostEstimate(**row_cost),
        name="col_pass_b",
    )(order, v, tiles)


def ring(k):
    return [(i, (i // 4) * 4 + (i + k) % 4) for i in range(SIDE)]


def hop(k):
    return [(i, (i + 4 * k) % SIDE) for i in range(SIDE)]


def swap(bits):
    return [(i, i ^ bits) for i in range(SIDE)]


def fast_form(x, y, lw, g, entries, count):
    xp, yp, x_sq, y_sq, order = pack(count, entries, x, y, lw, g)
    xz = jnp.stack([xp] + [lax.ppermute(xp, "tgt", swap(4 * k)) for k in (1, 2, 3)])
    yh = jnp.stack([yp, lax.ppermute(yp, "src", swap(2))])
    x1 = lax.ppermute(xz, "tgt", ring(1))
    x3 = lax.ppermute(xz, "tgt", ring(3))
    yy = [yh] + [lax.ppermute(yh, "src", hop(k)) for k in (1, 3, 2)]
    x2 = lax.ppermute(x1, "tgt", ring(1))
    ys = [z for a in yy for z in (a, lax.ppermute(a, "src", swap(1)))]

    ya, ub, tiles, acc, aux, stat = first_pass(order, (xz, x1, x3), ys)
    tiles, total, aux = second_pass(order, x2, ya, ub, tiles, acc, aux, stat)

    one, two, three = [lax.ppermute(total, "tgt", swap(k)) for k in (1, 2, 3)]
    total = (three + one) + (total + two)
    one, two, three = [lax.ppermute(total, "tgt", swap(4 * k)) for k in (1, 2, 3)]
    total = (one + two) + (total + three)

    f_own, v, away = far_pass(order, total, aux, x_sq, tiles)
    from_far = lax.ppermute(away, "src", swap(2))
    part = near_pass(order, v, tiles) + from_far
    part = part[0:4] + lax.ppermute(part[4:8], "src", swap(1))
    one, other, across = [
        lax.ppermute(part[k : k + 1], "src", swap(bits)) for k, bits in ((1, 4), (2, 12), (3, 8))
    ]
    part = (other + one) + (part[0:1] + across)
    offset = epsilon * ln2 * stat[1] + y_sq.reshape(BLOCK)
    return f_own.reshape(BLOCK), part.reshape(BLOCK), offset


def on_device(
    source_points, target_points, source_logw, target_logw, potential_in, pair_list, pair_counts
):
    f_own, t_own, offset = fast_form(
        source_points, target_points, source_logw, potential_in, pair_list[0], pair_counts
    )
    g_own = epsilon * target_logw - epsilon * jnp.log(t_own) + offset
    out_of_range = jnp.isnan(t_own[0])
    return lax.cond(
        out_of_range,
        plain_form,
        lambda *_: (f_own, g_own),
        source_points, target_points, source_logw, target_logw, potential_in, pair_list, pair_counts,
    )


def solution(mesh):
    return jax.shard_map(
        on_device,
        mesh=mesh,
        in_specs=(
            P(None, ("src", "tgt")),
            P(None, ("src", "tgt")),
            P(("src", "tgt")),
            P(("src", "tgt")),
            P(("src", "tgt")),
            P(("src", "tgt"), None, None),
            P(("src", "tgt")),
        ),
        out_specs=(P(("src", "tgt")), P(("src", "tgt"))),
        check_vma=False,
    )
```

```python
import functools

import jax
import jax.numpy as jnp
from jax import lax
from jax.experimental import pallas as pl
from jax.experimental.pallas import tpu as pltpu
from jax.sharding import PartitionSpec as P

epsilon = 0.25
lowest_log = -1e30
log2e = 1.4426950408889634
ln2 = 0.6931471805599453
SIDE = 16
BLOCK = 256
FEAT = 64
ROWS = 72
UNROLL = 8
vmem_bytes = 24 * 1024 * 1024
full_tiles = 128


def merge_pair(first, second):
    highest = jnp.maximum(first[0], second[0])
    summed = first[1] * jnp.exp(first[0] - highest) + second[1] * jnp.exp(second[0] - highest)
    return (highest, summed)


def cross_cost(left_all, left_sq, row_id, right_all, right_sq, col_id, block_len):
    left_points = lax.dynamic_slice_in_dim(left_all, row_id * block_len, block_len, 1)
    right_points = lax.dynamic_slice_in_dim(right_all, col_id * block_len, block_len, 1)
    left_norm = lax.dynamic_slice_in_dim(left_sq, row_id * block_len, block_len, 0)
    right_norm = lax.dynamic_slice_in_dim(right_sq, col_id * block_len, block_len, 0)
    inner_prod = lax.dot_general(
        left_points,
        right_points,
        (((0,), (0,)), ((), ())),
        precision=lax.Precision.HIGHEST,
        preferred_element_type=jnp.float32,
    )
    return left_norm[:, None] + right_norm[None, :] - 2.0 * inner_prod


def fold_part(running, position, highest, summed):
    old_high = lax.dynamic_slice_in_dim(running[0], position, 1, 0)[0]
    old_sum = lax.dynamic_slice_in_dim(running[1], position, 1, 0)[0]
    new_high, new_sum = merge_pair((old_high, old_sum), (highest, summed))
    return (
        lax.dynamic_update_slice_in_dim(running[0], new_high[None, :], position, 0),
        lax.dynamic_update_slice_in_dim(running[1], new_sum[None, :], position, 0),
    )


def gather_blocks(points, axis):
    copies = jnp.broadcast_to(points, (lax.axis_size(axis), *points.shape))
    blocks = lax.all_to_all(copies, axis, 0, 0, tiled=True)
    return jnp.moveaxis(blocks, 0, 1).reshape(points.shape[0], -1)


def plain_form(
    source_points, target_points, source_logw, target_logw, potential_in, pair_list, pair_counts
):
    n_tgt = lax.axis_size("tgt")
    n_src = lax.axis_size("src")
    block_len = source_points.shape[1]
    group_points = gather_blocks(source_points, "tgt")
    group_logw = lax.all_gather(source_logw, "tgt", axis=0, tiled=True)
    column_points = gather_blocks(target_points, "src")
    column_g = lax.all_gather(potential_in, "src", axis=0, tiled=True)
    group_sq = jnp.sum(group_points * group_points, axis=0)
    column_sq = jnp.sum(column_points * column_points, axis=0)
    row_start = (
        jnp.full((n_tgt, block_len), lowest_log, dtype=jnp.float32),
        jnp.zeros((n_tgt, block_len), dtype=jnp.float32),
    )
    col_start = (
        jnp.full((n_src, block_len), lowest_log, dtype=jnp.float32),
        jnp.zeros((n_src, block_len), dtype=jnp.float32),
    )
    own_entries = pair_list[0]
    own_count = pair_counts[0]

    def row_visit_pair(slot_id, carry):
        row_id = own_entries[slot_id, 0] % n_tgt
        col_id = own_entries[slot_id, 1] // n_tgt
        tile_cost = cross_cost(
            group_points, group_sq, row_id, column_points, column_sq, col_id, block_len
        )
        g_piece = lax.dynamic_slice_in_dim(column_g, col_id * block_len, block_len, 0)
        scores = (g_piece[None, :] - tile_cost) / epsilon
        highest = jnp.max(scores, axis=1)
        summed = jnp.sum(jnp.exp(scores - highest[:, None]), axis=1)
        return fold_part(carry, row_id, highest, summed)

    row_parts = lax.fori_loop(0, own_count, row_visit_pair, row_start)
    row_high = lax.pmax(row_parts[0], "tgt")
    row_sum = lax.psum(row_parts[1] * jnp.exp(row_parts[0] - row_high), "tgt")
    f_group = epsilon * group_logw - epsilon * (row_high + jnp.log(row_sum)).reshape(-1)
    f_own = lax.dynamic_slice_in_dim(f_group, lax.axis_index("tgt") * block_len, block_len, 0)

    def col_visit_pair(slot_id, carry):
        row_id = own_entries[slot_id, 0] % n_tgt
        col_id = own_entries[slot_id, 1] // n_tgt
        tile_cost = cross_cost(
            group_points, group_sq, row_id, column_points, column_sq, col_id, block_len
        )
        f_piece = lax.dynamic_slice_in_dim(f_group, row_id * block_len, block_len, 0)
        scores = (f_piece[:, None] - tile_cost) / epsilon
        highest = jnp.max(scores, axis=0)
        summed = jnp.sum(jnp.exp(scores - highest[None, :]), axis=0)
        return fold_part(carry, col_id, highest, summed)

    col_parts = lax.fori_loop(0, own_count, col_visit_pair, col_start)
    col_high = lax.pmax(col_parts[0], "src")
    col_sum = lax.psum(col_parts[1] * jnp.exp(col_parts[0] - col_high), "src")
    own_high = lax.dynamic_slice_in_dim(col_high, lax.axis_index("src"), 1, 0)[0]
    own_sum = lax.dynamic_slice_in_dim(col_sum, lax.axis_index("src"), 1, 0)[0]
    g_own = epsilon * target_logw - epsilon * (own_high + jnp.log(own_sum))
    return (f_own, g_own)


vmem = pl.BlockSpec(memory_space=pltpu.VMEM)


def f32(*shape):
    return jax.ShapeDtypeStruct(shape, jnp.float32)


def pack_kernel(
    count_ref, ent_ref, x_ref, y_ref, lw_ref, g_ref, xp_ref, yp_ref, xsq_ref, ysq_ref, out_ref
):
    x = x_ref[...]
    y = y_ref[...]
    y_sq = jnp.sum(y * y, axis=0, keepdims=True)
    b = (4.0 * log2e) * (g_ref[...] - y_sq)
    row = lax.broadcasted_iota(jnp.int32, (8, BLOCK), 0)
    b_max = jnp.max(b, axis=1, keepdims=True)
    xp_ref[0:FEAT, :] = x
    xp_ref[FEAT:ROWS, :] = jnp.where(row == 0, lw_ref[...], b_max)
    yp_ref[0:FEAT, :] = y
    yp_ref[FEAT:ROWS, :] = jnp.broadcast_to(b, (8, BLOCK))
    xsq_ref[...] = jnp.sum(x * x, axis=0, keepdims=True)
    ysq_ref[...] = y_sq
    tgt_id, src_id, count = lax.axis_index("tgt"), lax.axis_index("src"), count_ref[...]
    my_z, my_x = tgt_id // 4, tgt_id % 4
    my_y, my_h, my_c = src_id // 4, (src_id // 2) % 2, src_id % 2
    lane = lax.broadcasted_iota(jnp.int32, (1, full_tiles), 1)
    live = lane < count

    def ordered(key, code):
        tall = jnp.broadcast_to(key, (full_tiles, full_tiles)).T
        rank = jnp.sum(jnp.where(tall < key, 1, 0), axis=0, keepdims=True)
        spot = jnp.broadcast_to(rank, (full_tiles, full_tiles)).T
        tall_code = jnp.broadcast_to(code, (full_tiles, full_tiles)).T
        return jnp.sum(jnp.where(spot == lane, tall_code, 0), axis=0, keepdims=True)

    def how_many(mask):
        return jnp.sum(jnp.where(mask, 1, 0), axis=1, keepdims=True)

    row = ent_ref[0:1, :] & 15
    col = ent_ref[1:2, :] >> 4
    q = (my_x - (row & 3)) & 3
    p = my_z ^ (row >> 2)
    h = ((col >> 1) & 1) ^ my_h
    c = (col & 1) ^ my_c
    turn = (my_y - (col >> 2)) & 3
    yat = (turn ^ (turn >> 1)) * 4 + c * 2 + h
    dy = (col >> 2) ^ my_y
    spot = h * 8 + c * 4 + (dy ^ (dy >> 1))
    stage = jnp.where(q == 2, 1, 0)
    code = row + spot * 16 + (q * 4 + p) * 256 + yat * 4096
    code = ordered(jnp.where(live, stage, 3) * 128 + lane, jnp.where(live, code, 0))
    far = (code & 128) != 0
    code_b = (code & 127) + lane * 256
    code_b = ordered(jnp.where(live, jnp.where(far, 0, 1), 2) * 128 + lane, code_b)
    out_ref[0:1, :] = code
    out_ref[1:2, :] = code_b
    first = how_many(live & (stage == 0))
    away = how_many(live & far)
    out_ref[2:3, :] = jnp.where(lane == 0, first, jnp.where(lane == 2, away, count))
    out_ref[3:8, :] = jnp.zeros((5, full_tiles), jnp.int32)


def pack(count, entries, x, y, lw, g):
    return pl.pallas_call(
        pack_kernel,
        out_shape=(
            pltpu.VMEM((ROWS, BLOCK), jnp.float32), pltpu.VMEM((ROWS, BLOCK), jnp.float32),
            pltpu.VMEM((1, BLOCK), jnp.float32), pltpu.VMEM((1, BLOCK), jnp.float32),
            pltpu.VMEM((8, full_tiles), jnp.int32),
        ),
        in_specs=[vmem] * 6,
        out_specs=[vmem] * 5,
        name="pack",
    )(count.reshape(1, 1), entries.T, x, y, lw.reshape(1, BLOCK), g.reshape(1, BLOCK))


def prepare_source(x, at, xa):
    x = x * (8.0 * log2e)
    hi = x.astype(jnp.bfloat16)
    lo = (x - hi.astype(jnp.float32)).astype(jnp.bfloat16)
    xa[at, 0:64, :] = hi
    xa[at, 64:128, :] = lo
    xa[at, 128:192, :] = hi
    xa[at, 192:256, :] = lo


def note_source(block, q, p, aux_ref):
    tgt_id = lax.axis_index("tgt")
    where = ((tgt_id // 4) ^ p) * 4 + ((tgt_id % 4 - q) & 3)
    mean = jnp.sum(block[0:FEAT], axis=1, keepdims=True) * (1.0 / BLOCK)
    aux_ref[pl.ds(where, 1), :] = block[FEAT : FEAT + 1]
    aux_ref[16:17, :] = jnp.maximum(aux_ref[16:17, :], block[FEAT + 1 : FEAT + 2])
    aux_ref[17:18, :] = jnp.maximum(aux_ref[17:18, :], jnp.sum(mean * mean, axis=0, keepdims=True))


def visit_tiles(unroll, plan_ref, begin, end, xa, ya, ub, k_ref, acc_ref):
    def group(step, carry):
        for u in range(unroll):
            raw = begin + step * unroll + u
            slot = jnp.minimum(raw, end - 1)
            code = plan_ref[0, slot]
            xat = (code >> 8) & 15
            yat = (code >> 12) & 15
            row = code & 15
            scores = jnp.dot(ya[yat], xa[xat], preferred_element_type=jnp.float32)
            tile = jnp.exp2(scores)
            k_ref[slot] = tile.astype(jnp.bfloat16)
            weight = ub[yat]
            left = jnp.sum((tile[:, 0:128] * weight).reshape(32, 8, 128), axis=0)
            right = jnp.sum((tile[:, 128:256] * weight).reshape(32, 8, 128), axis=0)
            live = raw < end
            acc_ref[row, :, 0:128] += jnp.where(live, left, 0.0)
            acc_ref[row, :, 128:256] += jnp.where(live, right, 0.0)
        return carry

    lax.fori_loop(0, pl.cdiv(end - begin, unroll), group, 0)


def first_kernel(
    plan_ref, x0, x1, x3, y0, z0, y1, z1, y2, z2, y3, z3,
    ya, ub, k_ref, acc_ref, aux_ref, stat_ref, xa, codes, sem,
):
    fetch = pltpu.make_async_copy(plan_ref, codes, sem)
    fetch.start()
    ys = (y0, z0, y1, z1, y2, z2, y3, z3)
    lines = [ys[at // 2][at % 2, FEAT : FEAT + 1, :] for at in range(SIDE)]
    top = jnp.max(functools.reduce(jnp.maximum, lines), axis=1, keepdims=True)
    low = jnp.min(functools.reduce(jnp.minimum, lines), axis=1, keepdims=True) - top
    y_sq = jnp.zeros((1, BLOCK), jnp.float32)
    for at in range(SIDE):
        y = ys[at // 2][at % 2, 0:FEAT, :]
        y_sq = jnp.maximum(y_sq, jnp.sum(y * y, axis=0, keepdims=True))
        turned = jnp.concatenate([y, y], axis=0).T
        hi = turned.astype(jnp.bfloat16)
        lo = (turned - hi.astype(jnp.float32)).astype(jnp.bfloat16)
        ya[at, :, 0:128] = hi
        ya[at, :, 128:256] = lo
        ub[at] = jnp.broadcast_to(jnp.exp2(lines[at] - top), (128, BLOCK)).T
    stat_ref[0:1, :] = jnp.broadcast_to(low, (1, BLOCK))
    stat_ref[1:2, :] = jnp.broadcast_to(top, (1, BLOCK))
    stat_ref[2:3, :] = y_sq
    stat_ref[3:8, :] = jnp.zeros((5, BLOCK), jnp.float32)
    aux_ref[0:16, :] = jnp.zeros((16, BLOCK), jnp.float32)
    aux_ref[16:17, :] = jnp.full((1, BLOCK), -1e30, jnp.float32)
    aux_ref[17:24, :] = jnp.zeros((7, BLOCK), jnp.float32)
    for q, ref in ((0, x0), (1, x1), (3, x3)):
        for p in range(4):
            block = ref[p]
            prepare_source(block[0:FEAT], q * 4 + p, xa)
            note_source(block, q, p, aux_ref)
    acc_ref[...] = jnp.zeros_like(acc_ref)
    fetch.wait()
    visit_tiles(2 * UNROLL, codes, 0, codes[2, 0], xa, ya, ub, k_ref, acc_ref)


def second_kernel(
    plan_ref, x2, ya, ub, k_in, acc_in, aux_in, stat_ref,
    k_ref, s_ref, aux_ref, xa, acc, codes, sem,
):
    fetch = pltpu.make_async_copy(plan_ref, codes, sem)
    fetch.start()
    aux_ref[...] = aux_in[...]
    acc[...] = acc_in[...]
    for p in range(4):
        block = x2[p]
        prepare_source(block[0:FEAT], 8 + p, xa)
        note_source(block, 2, p, aux_ref)
    fetch.wait()
    visit_tiles(UNROLL, codes, codes[2, 0], codes[2, 3], xa, ya, ub, k_ref, acc)
    total = jnp.sum(acc[...], axis=1)
    low = stat_ref[0:1, 0:1]
    top = stat_ref[1:2, 0:1]
    shift = aux_ref[16:17, 0:1]
    lean = (8.0 * log2e) * jnp.sqrt(aux_ref[17:18, 0:1] * jnp.max(stat_ref[2:3, :], axis=1, keepdims=True))
    most = jnp.max(jnp.max(total, axis=0, keepdims=True), axis=1, keepdims=True)
    apart = top - shift
    good = (
        (lean <= 24.0)
        & (low >= -105.0)
        & (jnp.abs(apart) <= 16.0)
        & (most <= jnp.exp2(120.0 + low))
    )
    s_ref[...] = jnp.where(good, total * jnp.exp2(apart), jnp.nan)
    aux_ref[18:19, :] = jnp.broadcast_to(apart, (1, BLOCK))


tiles_shape = pltpu.VMEM((full_tiles, BLOCK, BLOCK), jnp.bfloat16)
target_shape = pltpu.VMEM((SIDE, BLOCK, BLOCK), jnp.bfloat16)
weight_shape = pltpu.VMEM((SIDE, BLOCK, 128), jnp.float32)
row_cost = dict(flops=32 * 2 * BLOCK**3, bytes_accessed=1 << 20, transcendentals=32 * BLOCK * BLOCK)


codes_scratch = [pltpu.SMEM((8, full_tiles), jnp.int32), pltpu.SemaphoreType.DMA]


def source_scratch(blocks):
    return pltpu.VMEM((blocks, BLOCK, BLOCK), jnp.bfloat16)


def first_pass(order, xs, ys):
    return pl.pallas_call(
        first_kernel,
        out_shape=(
            target_shape, weight_shape, tiles_shape,
            f32(SIDE, 8, BLOCK), f32(24, BLOCK), f32(8, BLOCK),
        ),
        in_specs=[vmem] * 12,
        out_specs=[vmem] * 6,
        scratch_shapes=[source_scratch(SIDE), *codes_scratch],
        compiler_params=pltpu.CompilerParams(vmem_limit_bytes=vmem_bytes),
        cost_estimate=pl.CostEstimate(**row_cost),
        name="row_pass_a",
    )(order, *xs, *ys)


def second_pass(order, x2, ya, ub, tiles, acc, aux, stat):
    return pl.pallas_call(
        second_kernel,
        out_shape=(tiles_shape, f32(SIDE, BLOCK), f32(24, BLOCK)),
        in_specs=[vmem] * 8,
        out_specs=[vmem] * 3,
        scratch_shapes=[source_scratch(SIDE), pltpu.VMEM((SIDE, 8, BLOCK), jnp.float32), *codes_scratch],
        input_output_aliases={4: 0},
        compiler_params=pltpu.CompilerParams(vmem_limit_bytes=vmem_bytes),
        cost_estimate=pl.CostEstimate(**row_cost),
        name="row_pass_b",
    )(order, x2, ya, ub, tiles, acc, aux, stat)


def visit_columns(plan_ref, begin, end, v_ref, k_ref, t_ref, acc):
    acc[...] = jnp.zeros_like(acc)

    def group(step, carry):
        for u in range(UNROLL):
            raw = begin + step * UNROLL + u
            code = plan_ref[1, jnp.minimum(raw, end - 1)]
            v = jnp.where(raw < end, v_ref[pl.ds(code & 15, 1), :], 0.0)
            tile = k_ref[code >> 8].astype(jnp.float32)
            acc[(code >> 4) & 7] += tile[:, 0:128] * v[:, 0:128] + tile[:, 128:256] * v[:, 128:256]
        return carry

    lax.fori_loop(0, pl.cdiv(end - begin, UNROLL), group, 0)
    ones = jnp.ones((16, 128), jnp.bfloat16)
    across = (((1,), (1,)), ((), ()))
    for c in range(8):
        rest = acc[c]
        total = jnp.zeros((16, BLOCK), jnp.float32)
        for _ in range(3):
            part = rest.astype(jnp.bfloat16)
            rest = rest - part.astype(jnp.float32)
            total += lax.dot_general(ones, part, across, preferred_element_type=jnp.float32)
        t_ref[c : c + 1, :] = total[0:1, :]


def far_kernel(plan_ref, s_ref, aux_ref, xsq_ref, k_ref, f_ref, v_ref, t_ref, acc, codes, sem):
    fetch = pltpu.make_async_copy(plan_ref, codes, sem)
    fetch.start()
    total = s_ref[...]
    v = jnp.exp(aux_ref[0:16, :]) / total * jnp.exp2(aux_ref[18:19, :])
    fine = jnp.where((total >= 1.5e-11) & (total <= 4.3e12), 1.0, 0.0)
    fine = jnp.min(jnp.min(fine, axis=1, keepdims=True), axis=0, keepdims=True) > 0.5
    v_ref[...] = jnp.where(fine, v, jnp.nan)
    own = lax.axis_index("tgt")
    own_s = s_ref[pl.ds(own, 1), :]
    own_lw = aux_ref[pl.ds(own, 1), :]
    f_ref[...] = epsilon * own_lw - epsilon * (jnp.log(own_s) + ln2 * aux_ref[16:17, :]) + xsq_ref[...]
    fetch.wait()
    visit_columns(codes, 0, codes[2, 2], v_ref, k_ref, t_ref, acc)
    t_ref[...] += jnp.where(fine, 0.0, jnp.nan)


def near_kernel(plan_ref, v_ref, k_ref, t_ref, acc, codes, sem):
    fetch = pltpu.make_async_copy(plan_ref, codes, sem)
    fetch.start()
    fetch.wait()
    visit_columns(codes, codes[2, 2], codes[2, 3], v_ref, k_ref, t_ref, acc)


def far_pass(order, total, aux, xsq, tiles):
    return pl.pallas_call(
        far_kernel,
        out_shape=(f32(1, BLOCK), f32(SIDE, BLOCK), f32(8, BLOCK)),
        in_specs=[vmem] * 5,
        out_specs=[vmem] * 3,
        scratch_shapes=[pltpu.VMEM((8, BLOCK, 128), jnp.float32), *codes_scratch],
        compiler_params=pltpu.CompilerParams(vmem_limit_bytes=vmem_bytes),
        cost_estimate=pl.CostEstimate(**row_cost),
        name="col_pass_a",
    )(order, total, aux, xsq, tiles)


def near_pass(order, v, tiles):
    return pl.pallas_call(
        near_kernel,
        out_shape=f32(8, BLOCK),
        in_specs=[vmem] * 3,
        out_specs=vmem,
        scratch_shapes=[pltpu.VMEM((8, BLOCK, 128), jnp.float32), *codes_scratch],
        compiler_params=pltpu.CompilerParams(vmem_limit_bytes=vmem_bytes),
        cost_estimate=pl.CostEstimate(**row_cost),
        name="col_pass_b",
    )(order, v, tiles)


def ring(k):
    return [(i, (i // 4) * 4 + (i + k) % 4) for i in range(SIDE)]


def hop(k):
    return [(i, (i + 4 * k) % SIDE) for i in range(SIDE)]


def swap(bits):
    return [(i, i ^ bits) for i in range(SIDE)]


def fast_form(x, y, lw, g, entries, count):
    xp, yp, x_sq, y_sq, order = pack(count, entries, x, y, lw, g)
    xz = jnp.stack([xp] + [lax.ppermute(xp, "tgt", swap(4 * k)) for k in (1, 2, 3)])
    yh = jnp.stack([yp, lax.ppermute(yp, "src", swap(2))])
    x1 = lax.ppermute(xz, "tgt", ring(1))
    x3 = lax.ppermute(xz, "tgt", ring(3))
    yy = [yh] + [lax.ppermute(yh, "src", hop(k)) for k in (1, 3, 2)]
    x2 = lax.ppermute(x1, "tgt", ring(1))
    ys = [z for a in yy for z in (a, lax.ppermute(a, "src", swap(1)))]

    ya, ub, tiles, acc, aux, stat = first_pass(order, (xz, x1, x3), ys)
    tiles, total, aux = second_pass(order, x2, ya, ub, tiles, acc, aux, stat)

    one, two, three = [lax.ppermute(total, "tgt", swap(k)) for k in (1, 2, 3)]
    total = (three + one) + (total + two)
    one, two, three = [lax.ppermute(total, "tgt", swap(4 * k)) for k in (1, 2, 3)]
    total = (one + two) + (total + three)

    f_own, v, away = far_pass(order, total, aux, x_sq, tiles)
    from_far = lax.ppermute(away, "src", swap(2))
    part = near_pass(order, v, tiles) + from_far
    part = part[0:4] + lax.ppermute(part[4:8], "src", swap(1))
    one, other, across = [
        lax.ppermute(part[k : k + 1], "src", swap(bits)) for k, bits in ((1, 4), (2, 12), (3, 8))
    ]
    part = (other + one) + (part[0:1] + across)
    offset = epsilon * ln2 * stat[1] + y_sq.reshape(BLOCK)
    return f_own.reshape(BLOCK), part.reshape(BLOCK), offset


def on_device(
    source_points, target_points, source_logw, target_logw, potential_in, pair_list, pair_counts
):
    f_own, t_own, offset = fast_form(
        source_points, target_points, source_logw, potential_in, pair_list[0], pair_counts
    )
    g_own = epsilon * target_logw - epsilon * jnp.log(t_own) + offset
    out_of_range = jnp.isnan(t_own[0])
    return lax.cond(
        out_of_range,
        plain_form,
        lambda *_: (f_own, g_own),
        source_points, target_points, source_logw, target_logw, potential_in, pair_list, pair_counts,
    )


def solution(mesh):
    return jax.shard_map(
        on_device,
        mesh=mesh,
        in_specs=(
            P(None, ("src", "tgt")),
            P(None, ("src", "tgt")),
            P(("src", "tgt")),
            P(("src", "tgt")),
            P(("src", "tgt")),
            P(("src", "tgt"), None, None),
            P(("src", "tgt")),
        ),
        out_specs=(P(("src", "tgt")), P(("src", "tgt"))),
        check_vma=False,
    )
```

```python
import functools

import jax
import jax.numpy as jnp
from jax import lax
from jax.experimental import pallas as pl
from jax.experimental.pallas import tpu as pltpu
from jax.sharding import PartitionSpec as P

epsilon = 0.25
lowest_log = -1e30
log2e = 1.4426950408889634
ln2 = 0.6931471805599453
SIDE = 16
BLOCK = 256
FEAT = 64
ROWS = 72
UNROLL = 8
vmem_bytes = 24 * 1024 * 1024
full_tiles = 128


def merge_pair(first, second):
    highest = jnp.maximum(first[0], second[0])
    summed = first[1] * jnp.exp(first[0] - highest) + second[1] * jnp.exp(second[0] - highest)
    return (highest, summed)


def cross_cost(left_all, left_sq, row_id, right_all, right_sq, col_id, block_len):
    left_points = lax.dynamic_slice_in_dim(left_all, row_id * block_len, block_len, 1)
    right_points = lax.dynamic_slice_in_dim(right_all, col_id * block_len, block_len, 1)
    left_norm = lax.dynamic_slice_in_dim(left_sq, row_id * block_len, block_len, 0)
    right_norm = lax.dynamic_slice_in_dim(right_sq, col_id * block_len, block_len, 0)
    inner_prod = lax.dot_general(
        left_points,
        right_points,
        (((0,), (0,)), ((), ())),
        precision=lax.Precision.HIGHEST,
        preferred_element_type=jnp.float32,
    )
    return left_norm[:, None] + right_norm[None, :] - 2.0 * inner_prod


def fold_part(running, position, highest, summed):
    old_high = lax.dynamic_slice_in_dim(running[0], position, 1, 0)[0]
    old_sum = lax.dynamic_slice_in_dim(running[1], position, 1, 0)[0]
    new_high, new_sum = merge_pair((old_high, old_sum), (highest, summed))
    return (
        lax.dynamic_update_slice_in_dim(running[0], new_high[None, :], position, 0),
        lax.dynamic_update_slice_in_dim(running[1], new_sum[None, :], position, 0),
    )


def gather_blocks(points, axis):
    copies = jnp.broadcast_to(points, (lax.axis_size(axis), *points.shape))
    blocks = lax.all_to_all(copies, axis, 0, 0, tiled=True)
    return jnp.moveaxis(blocks, 0, 1).reshape(points.shape[0], -1)


def plain_form(
    source_points, target_points, source_logw, target_logw, potential_in, pair_list, pair_counts
):
    n_tgt = lax.axis_size("tgt")
    n_src = lax.axis_size("src")
    block_len = source_points.shape[1]
    group_points = gather_blocks(source_points, "tgt")
    group_logw = lax.all_gather(source_logw, "tgt", axis=0, tiled=True)
    column_points = gather_blocks(target_points, "src")
    column_g = lax.all_gather(potential_in, "src", axis=0, tiled=True)
    group_sq = jnp.sum(group_points * group_points, axis=0)
    column_sq = jnp.sum(column_points * column_points, axis=0)
    row_start = (
        jnp.full((n_tgt, block_len), lowest_log, dtype=jnp.float32),
        jnp.zeros((n_tgt, block_len), dtype=jnp.float32),
    )
    col_start = (
        jnp.full((n_src, block_len), lowest_log, dtype=jnp.float32),
        jnp.zeros((n_src, block_len), dtype=jnp.float32),
    )
    own_entries = pair_list[0]
    own_count = pair_counts[0]

    def row_visit_pair(slot_id, carry):
        row_id = own_entries[slot_id, 0] % n_tgt
        col_id = own_entries[slot_id, 1] // n_tgt
        tile_cost = cross_cost(
            group_points, group_sq, row_id, column_points, column_sq, col_id, block_len
        )
        g_piece = lax.dynamic_slice_in_dim(column_g, col_id * block_len, block_len, 0)
        scores = (g_piece[None, :] - tile_cost) / epsilon
        highest = jnp.max(scores, axis=1)
        summed = jnp.sum(jnp.exp(scores - highest[:, None]), axis=1)
        return fold_part(carry, row_id, highest, summed)

    row_parts = lax.fori_loop(0, own_count, row_visit_pair, row_start)
    row_high = lax.pmax(row_parts[0], "tgt")
    row_sum = lax.psum(row_parts[1] * jnp.exp(row_parts[0] - row_high), "tgt")
    f_group = epsilon * group_logw - epsilon * (row_high + jnp.log(row_sum)).reshape(-1)
    f_own = lax.dynamic_slice_in_dim(f_group, lax.axis_index("tgt") * block_len, block_len, 0)

    def col_visit_pair(slot_id, carry):
        row_id = own_entries[slot_id, 0] % n_tgt
        col_id = own_entries[slot_id, 1] // n_tgt
        tile_cost = cross_cost(
            group_points, group_sq, row_id, column_points, column_sq, col_id, block_len
        )
        f_piece = lax.dynamic_slice_in_dim(f_group, row_id * block_len, block_len, 0)
        scores = (f_piece[:, None] - tile_cost) / epsilon
        highest = jnp.max(scores, axis=0)
        summed = jnp.sum(jnp.exp(scores - highest[None, :]), axis=0)
        return fold_part(carry, col_id, highest, summed)

    col_parts = lax.fori_loop(0, own_count, col_visit_pair, col_start)
    col_high = lax.pmax(col_parts[0], "src")
    col_sum = lax.psum(col_parts[1] * jnp.exp(col_parts[0] - col_high), "src")
    own_high = lax.dynamic_slice_in_dim(col_high, lax.axis_index("src"), 1, 0)[0]
    own_sum = lax.dynamic_slice_in_dim(col_sum, lax.axis_index("src"), 1, 0)[0]
    g_own = epsilon * target_logw - epsilon * (own_high + jnp.log(own_sum))
    return (f_own, g_own)


vmem = pl.BlockSpec(memory_space=pltpu.VMEM)


def f32(*shape):
    return jax.ShapeDtypeStruct(shape, jnp.float32)


def pack_kernel(
    count_ref, ent_ref, x_ref, y_ref, g_ref, lw_ref, yp_ref, xv_ref, xsq_ref, ysq_ref, lwv_ref, out_ref
):
    x = x_ref[...]
    xv_ref[...] = x
    lwv_ref[...] = lw_ref[...]
    y = y_ref[...]
    y_sq = jnp.sum(y * y, axis=0, keepdims=True)
    b = (4.0 * log2e) * (g_ref[...] - y_sq)
    yp_ref[0:FEAT, :] = y
    yp_ref[FEAT:ROWS, :] = jnp.broadcast_to(b, (8, BLOCK))
    xsq_ref[...] = jnp.sum(x * x, axis=0, keepdims=True)
    ysq_ref[...] = y_sq
    tgt_id, src_id, count = lax.axis_index("tgt"), lax.axis_index("src"), count_ref[...]
    my_z, my_x = tgt_id // 4, tgt_id % 4
    my_y, my_h, my_c = src_id // 4, (src_id // 2) % 2, src_id % 2
    lane = lax.broadcasted_iota(jnp.int32, (1, full_tiles), 1)
    live = lane < count

    def ordered(key, code):
        tall = jnp.broadcast_to(key, (full_tiles, full_tiles)).T
        rank = jnp.sum(jnp.where(tall < key, 1, 0), axis=0, keepdims=True)
        spot = jnp.broadcast_to(rank, (full_tiles, full_tiles)).T
        tall_code = jnp.broadcast_to(code, (full_tiles, full_tiles)).T
        return jnp.sum(jnp.where(spot == lane, tall_code, 0), axis=0, keepdims=True)

    def how_many(mask):
        return jnp.sum(jnp.where(mask, 1, 0), axis=1, keepdims=True)

    row = ent_ref[0:1, :] & 15
    col = ent_ref[1:2, :] >> 4
    q = (my_x - (row & 3)) & 3
    p = my_z ^ (row >> 2)
    h = ((col >> 1) & 1) ^ my_h
    c = (col & 1) ^ my_c
    turn = (my_y - (col >> 2)) & 3
    yat = (turn ^ (turn >> 1)) * 4 + c * 2 + h
    dy = (col >> 2) ^ my_y
    spot = h * 8 + c * 4 + (dy ^ (dy >> 1))
    stage = jnp.where(q == 2, 1, 0)
    code = row + spot * 16 + (q * 4 + p) * 256 + yat * 4096
    code = ordered(jnp.where(live, stage, 3) * 128 + lane, jnp.where(live, code, 0))
    far = (code & 128) != 0
    code_b = (code & 127) + lane * 256
    code_b = ordered(jnp.where(live, jnp.where(far, 0, 1), 2) * 128 + lane, code_b)
    out_ref[0:1, :] = code
    out_ref[1:2, :] = code_b
    first = how_many(live & (stage == 0))
    away = how_many(live & far)
    out_ref[2:3, :] = jnp.where(lane == 0, first, jnp.where(lane == 2, away, count))
    out_ref[3:8, :] = jnp.zeros((5, full_tiles), jnp.int32)


def pack(count, entries, x, y, g, lw):
    return pl.pallas_call(
        pack_kernel,
        out_shape=(
            pltpu.VMEM((ROWS, BLOCK), jnp.float32), pltpu.VMEM((FEAT, BLOCK), jnp.float32),
            pltpu.VMEM((1, BLOCK), jnp.float32), pltpu.VMEM((1, BLOCK), jnp.float32), pltpu.VMEM((1, BLOCK), jnp.float32),
            pltpu.VMEM((8, full_tiles), jnp.int32),
        ),
        in_specs=[vmem] * 6,
        out_specs=[vmem] * 6,
        name="pack",
    )(count.reshape(1, 1), entries.T, x, y, g.reshape(1, BLOCK), lw.reshape(1, BLOCK))


def prepare_source(x, at, xa):
    x = x * (8.0 * log2e)
    hi = x.astype(jnp.bfloat16)
    lo = (x - hi.astype(jnp.float32)).astype(jnp.bfloat16)
    xa[at, 0:64, :] = hi
    xa[at, 64:128, :] = lo
    xa[at, 128:192, :] = hi
    xa[at, 192:256, :] = lo


def mean_square(block):
    mean = jnp.sum(block, axis=1, keepdims=True) * (1.0 / BLOCK)
    return jnp.sum(mean * mean, axis=0, keepdims=True)


def visit_tiles(unroll, plan_ref, begin, end, xa, ya, ub, k_ref, acc_ref):
    def group(step, carry):
        for u in range(unroll):
            raw = begin + step * unroll + u
            slot = jnp.minimum(raw, end - 1)
            code = plan_ref[0, slot]
            xat = (code >> 8) & 15
            yat = (code >> 12) & 15
            row = code & 15
            scores = jnp.dot(ya[yat], xa[xat], preferred_element_type=jnp.float32)
            tile = jnp.exp2(scores)
            k_ref[slot] = tile.astype(jnp.bfloat16)
            weight = ub[yat]
            left = jnp.sum((tile[:, 0:128] * weight).reshape(32, 8, 128), axis=0)
            right = jnp.sum((tile[:, 128:256] * weight).reshape(32, 8, 128), axis=0)
            live = raw < end
            acc_ref[row, :, 0:128] += jnp.where(live, left, 0.0)
            acc_ref[row, :, 128:256] += jnp.where(live, right, 0.0)
        return carry

    lax.fori_loop(0, pl.cdiv(end - begin, unroll), group, 0)


def first_kernel(
    plan_ref, x0, x1, x3, y0, z0, y1, z1, y2, z2, y3, z3,
    ya, ub, k_ref, acc_ref, stat_ref, xa, codes, sem,
):
    fetch = pltpu.make_async_copy(plan_ref, codes, sem)
    fetch.start()
    ys = (y0, z0, y1, z1, y2, z2, y3, z3)
    lines = [ys[at // 2][at % 2, FEAT : FEAT + 1, :] for at in range(SIDE)]
    top = jnp.max(functools.reduce(jnp.maximum, lines), axis=1, keepdims=True)
    low = jnp.min(functools.reduce(jnp.minimum, lines), axis=1, keepdims=True) - top
    y_sq = jnp.zeros((1, BLOCK), jnp.float32)
    for at in range(SIDE):
        y = ys[at // 2][at % 2, 0:FEAT, :]
        y_sq = jnp.maximum(y_sq, jnp.sum(y * y, axis=0, keepdims=True))
        turned = jnp.concatenate([y, y], axis=0).T
        hi = turned.astype(jnp.bfloat16)
        lo = (turned - hi.astype(jnp.float32)).astype(jnp.bfloat16)
        ya[at, :, 0:128] = hi
        ya[at, :, 128:256] = lo
        ub[at] = jnp.broadcast_to(jnp.exp2(lines[at] - top), (128, BLOCK)).T
    stat_ref[0:1, :] = jnp.broadcast_to(low, (1, BLOCK))
    stat_ref[1:2, :] = jnp.broadcast_to(top, (1, BLOCK))
    stat_ref[2:3, :] = y_sq
    x_mean = jnp.zeros((1, 1), jnp.float32)
    for q, ref in ((0, x0), (1, x1), (3, x3)):
        for p in range(4):
            block = ref[p]
            prepare_source(block, q * 4 + p, xa)
            x_mean = jnp.maximum(x_mean, mean_square(block))
    stat_ref[3:4, :] = jnp.broadcast_to(x_mean, (1, BLOCK))
    stat_ref[4:8, :] = jnp.zeros((4, BLOCK), jnp.float32)
    acc_ref[...] = jnp.zeros_like(acc_ref)
    fetch.wait()
    visit_tiles(2 * UNROLL, codes, 0, codes[2, 0], xa, ya, ub, k_ref, acc_ref)


def second_kernel(
    plan_ref, x2, ya, ub, k_in, acc_in, stat_ref, lw_ref, k_ref, s_ref, xa, acc, codes, sem
):
    fetch = pltpu.make_async_copy(plan_ref, codes, sem)
    fetch.start()
    acc[...] = acc_in[...]
    x_mean = stat_ref[3:4, 0:1]
    for p in range(4):
        block = x2[p]
        prepare_source(block, 8 + p, xa)
        x_mean = jnp.maximum(x_mean, mean_square(block))
    fetch.wait()
    visit_tiles(UNROLL, codes, codes[2, 0], codes[2, 3], xa, ya, ub, k_ref, acc)
    total = jnp.sum(acc[...], axis=1)
    low = stat_ref[0:1, 0:1]
    lean = (8.0 * log2e) * jnp.sqrt(x_mean * jnp.max(stat_ref[2:3, :], axis=1, keepdims=True))
    most = jnp.max(jnp.max(total, axis=0, keepdims=True), axis=1, keepdims=True)
    good = (lean <= 24.0) & (low >= -105.0) & (most <= jnp.exp2(120.0 + low))
    s_ref[0:16, :] = jnp.where(good, total, jnp.nan)
    s_ref[16:17, :] = stat_ref[1:2, :]
    s_ref[17:18, :] = stat_ref[1:2, :]
    s_ref[18:19, :] = lw_ref[...]
    s_ref[19:24, :] = jnp.zeros((5, BLOCK), jnp.float32)


tiles_shape = pltpu.VMEM((full_tiles, BLOCK, BLOCK), jnp.bfloat16)
target_shape = pltpu.VMEM((SIDE, BLOCK, BLOCK), jnp.bfloat16)
weight_shape = pltpu.VMEM((SIDE, BLOCK, 128), jnp.float32)
row_cost = dict(flops=32 * 2 * BLOCK**3, bytes_accessed=1 << 20, transcendentals=32 * BLOCK * BLOCK)


codes_scratch = [pltpu.SMEM((8, full_tiles), jnp.int32), pltpu.SemaphoreType.DMA]


def source_scratch(blocks):
    return pltpu.VMEM((blocks, BLOCK, BLOCK), jnp.bfloat16)


def first_pass(order, xs, ys):
    return pl.pallas_call(
        first_kernel,
        out_shape=(
            target_shape, weight_shape, tiles_shape,
            f32(SIDE, 8, BLOCK), f32(8, BLOCK),
        ),
        in_specs=[vmem] * 12,
        out_specs=[vmem] * 5,
        scratch_shapes=[source_scratch(SIDE), *codes_scratch],
        compiler_params=pltpu.CompilerParams(vmem_limit_bytes=vmem_bytes),
        cost_estimate=pl.CostEstimate(**row_cost),
        name="row_pass_a",
    )(order, *xs, *ys)


def second_pass(order, x2, ya, ub, tiles, acc, stat, lw):
    return pl.pallas_call(
        second_kernel,
        out_shape=(tiles_shape, f32(24, BLOCK)),
        in_specs=[vmem] * 8,
        out_specs=[vmem] * 2,
        scratch_shapes=[source_scratch(SIDE), pltpu.VMEM((SIDE, 8, BLOCK), jnp.float32), *codes_scratch],
        input_output_aliases={4: 0},
        compiler_params=pltpu.CompilerParams(vmem_limit_bytes=vmem_bytes),
        cost_estimate=pl.CostEstimate(**row_cost),
        name="row_pass_b",
    )(order, x2, ya, ub, tiles, acc, stat, lw)


def visit_columns(plan_ref, begin, end, v_ref, k_ref, t_ref, acc):
    acc[...] = jnp.zeros_like(acc)

    def group(step, carry):
        for u in range(UNROLL):
            raw = begin + step * UNROLL + u
            code = plan_ref[1, jnp.minimum(raw, end - 1)]
            v = jnp.where(raw < end, v_ref[pl.ds(code & 15, 1), :], 0.0)
            tile = k_ref[code >> 8].astype(jnp.float32)
            acc[(code >> 4) & 7] += tile[:, 0:128] * v[:, 0:128] + tile[:, 128:256] * v[:, 128:256]
        return carry

    lax.fori_loop(0, pl.cdiv(end - begin, UNROLL), group, 0)
    ones = jnp.ones((16, 128), jnp.bfloat16)
    across = (((1,), (1,)), ((), ()))
    for c in range(8):
        rest = acc[c]
        total = jnp.zeros((16, BLOCK), jnp.float32)
        for _ in range(3):
            part = rest.astype(jnp.bfloat16)
            rest = rest - part.astype(jnp.float32)
            total += lax.dot_general(ones, part, across, preferred_element_type=jnp.float32)
        t_ref[c : c + 1, :] = total[0:1, :]


def far_kernel(
    plan_ref, s_ref, ends_ref, lw_ref, stat_ref, xsq_ref, k_ref, f_ref, v_ref, t_ref, acc, codes, sem
):
    fetch = pltpu.make_async_copy(plan_ref, codes, sem)
    fetch.start()
    total = s_ref[...]
    shift = ends_ref[0:1, :]
    own = lax.axis_index("tgt")
    for r in range(SIDE):
        off = (r // 4) * 4 + (0, 3, 1, 2)[r % 4]
        v_ref[pl.ds(own ^ off, 1), :] = lw_ref[r : r + 1, :]
    v = jnp.exp(v_ref[...]) / total * jnp.exp2(stat_ref[1:2, :] - shift)
    fine = (total >= 1.5e-11) & (total <= 4.3e12) & (shift - ends_ref[1:2, :] <= 16.0)
    fine = jnp.where(fine, 1.0, 0.0)
    fine = jnp.min(jnp.min(fine, axis=1, keepdims=True), axis=0, keepdims=True) > 0.5
    v_ref[...] = jnp.where(fine, v, jnp.nan)
    own_s = s_ref[pl.ds(own, 1), :]
    f_ref[...] = epsilon * lw_ref[0:1, :] - epsilon * (jnp.log(own_s) + ln2 * shift) + xsq_ref[...]
    fetch.wait()
    visit_columns(codes, 0, codes[2, 2], v_ref, k_ref, t_ref, acc)
    t_ref[...] += jnp.where(fine, 0.0, jnp.nan)


def near_kernel(plan_ref, v_ref, k_ref, t_ref, acc, codes, sem):
    fetch = pltpu.make_async_copy(plan_ref, codes, sem)
    fetch.start()
    fetch.wait()
    visit_columns(codes, codes[2, 2], codes[2, 3], v_ref, k_ref, t_ref, acc)


def far_pass(order, total, ends, lw, stat, xsq, tiles):
    return pl.pallas_call(
        far_kernel,
        out_shape=(f32(1, BLOCK), f32(SIDE, BLOCK), f32(8, BLOCK)),
        in_specs=[vmem] * 7,
        out_specs=[vmem] * 3,
        scratch_shapes=[pltpu.VMEM((8, BLOCK, 128), jnp.float32), *codes_scratch],
        compiler_params=pltpu.CompilerParams(vmem_limit_bytes=vmem_bytes),
        cost_estimate=pl.CostEstimate(**row_cost),
        name="col_pass_a",
    )(order, total, ends, lw, stat, xsq, tiles)


def near_pass(order, v, tiles):
    return pl.pallas_call(
        near_kernel,
        out_shape=f32(8, BLOCK),
        in_specs=[vmem] * 3,
        out_specs=vmem,
        scratch_shapes=[pltpu.VMEM((8, BLOCK, 128), jnp.float32), *codes_scratch],
        compiler_params=pltpu.CompilerParams(vmem_limit_bytes=vmem_bytes),
        cost_estimate=pl.CostEstimate(**row_cost),
        name="col_pass_b",
    )(order, v, tiles)


def ring(k):
    return [(i, (i // 4) * 4 + (i + k) % 4) for i in range(SIDE)]


def hop(k):
    return [(i, (i + 4 * k) % SIDE) for i in range(SIDE)]


def swap(bits):
    return [(i, i ^ bits) for i in range(SIDE)]


def stacked(rows, *pieces):
    out, at = 0.0, 0
    for piece in pieces:
        height = piece.shape[0]
        out = out + lax.pad(piece, jnp.float32(0.0), ((at, rows - at - height, 0), (0, 0, 0)))
        at += height
    return out


def one_scale(*parts_weights):
    *parts, weights = parts_weights
    high = functools.reduce(jnp.maximum, [p[16:17] for p in parts])
    low = functools.reduce(jnp.minimum, [p[17:18] for p in parts])
    scaled = lax.optimization_barrier([p[0:16] * jnp.exp2(p[16:17] - high) for p in parts])
    return scaled, stacked(2, high, low), stacked(4 * weights, *[p[18 : 18 + weights] for p in parts])


def fast_form(x, y, lw, g, entries, count):
    yp, own_x, x_sq, y_sq, lw, order = pack(count, entries, x, y, g, lw)
    xz = jnp.stack([own_x] + [lax.ppermute(x, "tgt", swap(4 * k)) for k in (1, 2, 3)])
    yh = jnp.stack([yp, lax.ppermute(yp, "src", swap(2))])
    x1 = lax.ppermute(xz, "tgt", ring(1))
    x3 = lax.ppermute(xz, "tgt", ring(3))
    yy = [yh] + [lax.ppermute(yh, "src", hop(k)) for k in (1, 3, 2)]
    x2 = lax.ppermute(x1, "tgt", ring(1))
    ys = [z for a in yy for z in (a, lax.ppermute(a, "src", swap(1)))]

    ya, ub, tiles, acc, stat = first_pass(order, (xz, x1, x3), ys)
    tiles, total = second_pass(order, x2, ya, ub, tiles, acc, stat, lw)

    one, two, three = [lax.ppermute(total, "tgt", swap(k)) for k in (1, 2, 3)]
    (a, d, b, c), ends, logs = one_scale(total, three, one, two, 1)
    total = stacked(24, (d + b) + (a + c), ends, logs)
    one, two, three = [lax.ppermute(total, "tgt", swap(4 * k)) for k in (1, 2, 3)]
    (a, b, c, d), ends, logs = one_scale(total, one, two, three, 4)
    total = (b + c) + (a + d)

    f_own, v, away = far_pass(order, total, ends, logs, stat, x_sq, tiles)
    from_far = lax.ppermute(away, "src", swap(2))
    part = near_pass(order, v, tiles) + from_far
    part = part[0:4] + lax.ppermute(part[4:8], "src", swap(1))
    one, other, across = [
        lax.ppermute(part[k : k + 1], "src", swap(bits)) for k, bits in ((1, 4), (2, 12), (3, 8))
    ]
    part = (other + one) + (part[0:1] + across)
    offset = epsilon * ln2 * stat[1] + y_sq.reshape(BLOCK)
    return f_own.reshape(BLOCK), part.reshape(BLOCK), offset


def on_device(
    source_points, target_points, source_logw, target_logw, potential_in, pair_list, pair_counts
):
    f_own, t_own, offset = fast_form(
        source_points, target_points, source_logw, potential_in, pair_list[0], pair_counts
    )
    g_own = epsilon * target_logw - epsilon * jnp.log(t_own) + offset
    out_of_range = jnp.isnan(t_own[0])
    return lax.cond(
        out_of_range,
        plain_form,
        lambda *_: (f_own, g_own),
        source_points, target_points, source_logw, target_logw, potential_in, pair_list, pair_counts,
    )


def solution(mesh):
    return jax.shard_map(
        on_device,
        mesh=mesh,
        in_specs=(
            P(None, ("src", "tgt")),
            P(None, ("src", "tgt")),
            P(("src", "tgt")),
            P(("src", "tgt")),
            P(("src", "tgt")),
            P(("src", "tgt"), None, None),
            P(("src", "tgt")),
        ),
        out_specs=(P(("src", "tgt")), P(("src", "tgt"))),
        check_vma=False,
    )
```

```python
import functools

import jax
import jax.numpy as jnp
from jax import lax
from jax.experimental import pallas as pl
from jax.experimental.pallas import tpu as pltpu
from jax.sharding import PartitionSpec as P

epsilon = 0.25
lowest_log = -1e30
log2e = 1.4426950408889634
ln2 = 0.6931471805599453
SIDE = 16
BLOCK = 256
FEAT = 64
ROWS = 72
UNROLL = 8
vmem_bytes = 24 * 1024 * 1024
full_tiles = 128


def merge_pair(first, second):
    highest = jnp.maximum(first[0], second[0])
    summed = first[1] * jnp.exp(first[0] - highest) + second[1] * jnp.exp(second[0] - highest)
    return (highest, summed)


def cross_cost(left_all, left_sq, row_id, right_all, right_sq, col_id, block_len):
    left_points = lax.dynamic_slice_in_dim(left_all, row_id * block_len, block_len, 1)
    right_points = lax.dynamic_slice_in_dim(right_all, col_id * block_len, block_len, 1)
    left_norm = lax.dynamic_slice_in_dim(left_sq, row_id * block_len, block_len, 0)
    right_norm = lax.dynamic_slice_in_dim(right_sq, col_id * block_len, block_len, 0)
    inner_prod = lax.dot_general(
        left_points,
        right_points,
        (((0,), (0,)), ((), ())),
        precision=lax.Precision.HIGHEST,
        preferred_element_type=jnp.float32,
    )
    return left_norm[:, None] + right_norm[None, :] - 2.0 * inner_prod


def fold_part(running, position, highest, summed):
    old_high = lax.dynamic_slice_in_dim(running[0], position, 1, 0)[0]
    old_sum = lax.dynamic_slice_in_dim(running[1], position, 1, 0)[0]
    new_high, new_sum = merge_pair((old_high, old_sum), (highest, summed))
    return (
        lax.dynamic_update_slice_in_dim(running[0], new_high[None, :], position, 0),
        lax.dynamic_update_slice_in_dim(running[1], new_sum[None, :], position, 0),
    )


def gather_blocks(points, axis):
    copies = jnp.broadcast_to(points, (lax.axis_size(axis), *points.shape))
    blocks = lax.all_to_all(copies, axis, 0, 0, tiled=True)
    return jnp.moveaxis(blocks, 0, 1).reshape(points.shape[0], -1)


def plain_form(
    source_points, target_points, source_logw, target_logw, potential_in, pair_list, pair_counts
):
    n_tgt = lax.axis_size("tgt")
    n_src = lax.axis_size("src")
    block_len = source_points.shape[1]
    group_points = gather_blocks(source_points, "tgt")
    group_logw = lax.all_gather(source_logw, "tgt", axis=0, tiled=True)
    column_points = gather_blocks(target_points, "src")
    column_g = lax.all_gather(potential_in, "src", axis=0, tiled=True)
    group_sq = jnp.sum(group_points * group_points, axis=0)
    column_sq = jnp.sum(column_points * column_points, axis=0)
    row_start = (
        jnp.full((n_tgt, block_len), lowest_log, dtype=jnp.float32),
        jnp.zeros((n_tgt, block_len), dtype=jnp.float32),
    )
    col_start = (
        jnp.full((n_src, block_len), lowest_log, dtype=jnp.float32),
        jnp.zeros((n_src, block_len), dtype=jnp.float32),
    )
    own_entries = pair_list[0]
    own_count = pair_counts[0]

    def row_visit_pair(slot_id, carry):
        row_id = own_entries[slot_id, 0] % n_tgt
        col_id = own_entries[slot_id, 1] // n_tgt
        tile_cost = cross_cost(
            group_points, group_sq, row_id, column_points, column_sq, col_id, block_len
        )
        g_piece = lax.dynamic_slice_in_dim(column_g, col_id * block_len, block_len, 0)
        scores = (g_piece[None, :] - tile_cost) / epsilon
        highest = jnp.max(scores, axis=1)
        summed = jnp.sum(jnp.exp(scores - highest[:, None]), axis=1)
        return fold_part(carry, row_id, highest, summed)

    row_parts = lax.fori_loop(0, own_count, row_visit_pair, row_start)
    row_high = lax.pmax(row_parts[0], "tgt")
    row_sum = lax.psum(row_parts[1] * jnp.exp(row_parts[0] - row_high), "tgt")
    f_group = epsilon * group_logw - epsilon * (row_high + jnp.log(row_sum)).reshape(-1)
    f_own = lax.dynamic_slice_in_dim(f_group, lax.axis_index("tgt") * block_len, block_len, 0)

    def col_visit_pair(slot_id, carry):
        row_id = own_entries[slot_id, 0] % n_tgt
        col_id = own_entries[slot_id, 1] // n_tgt
        tile_cost = cross_cost(
            group_points, group_sq, row_id, column_points, column_sq, col_id, block_len
        )
        f_piece = lax.dynamic_slice_in_dim(f_group, row_id * block_len, block_len, 0)
        scores = (f_piece[:, None] - tile_cost) / epsilon
        highest = jnp.max(scores, axis=0)
        summed = jnp.sum(jnp.exp(scores - highest[None, :]), axis=0)
        return fold_part(carry, col_id, highest, summed)

    col_parts = lax.fori_loop(0, own_count, col_visit_pair, col_start)
    col_high = lax.pmax(col_parts[0], "src")
    col_sum = lax.psum(col_parts[1] * jnp.exp(col_parts[0] - col_high), "src")
    own_high = lax.dynamic_slice_in_dim(col_high, lax.axis_index("src"), 1, 0)[0]
    own_sum = lax.dynamic_slice_in_dim(col_sum, lax.axis_index("src"), 1, 0)[0]
    g_own = epsilon * target_logw - epsilon * (own_high + jnp.log(own_sum))
    return (f_own, g_own)


vmem = pl.BlockSpec(memory_space=pltpu.VMEM)


def f32(*shape):
    return jax.ShapeDtypeStruct(shape, jnp.float32)


def pack_kernel(
    count_ref, ent_ref, x_ref, y_ref, g_ref, lw_ref, yp_ref, xv_ref, xsq_ref, ysq_ref, lwv_ref, out_ref
):
    x = x_ref[...]
    xv_ref[...] = x
    lwv_ref[...] = lw_ref[...]
    y = y_ref[...]
    y_sq = jnp.sum(y * y, axis=0, keepdims=True)
    b = (4.0 * log2e) * (g_ref[...] - y_sq)
    yp_ref[0:FEAT, :] = y
    yp_ref[FEAT:ROWS, :] = jnp.broadcast_to(b, (8, BLOCK))
    xsq_ref[...] = jnp.sum(x * x, axis=0, keepdims=True)
    ysq_ref[...] = y_sq
    tgt_id, src_id, count = lax.axis_index("tgt"), lax.axis_index("src"), count_ref[...]
    my_z, my_x = tgt_id // 4, tgt_id % 4
    my_y, my_h, my_c = src_id // 4, (src_id // 2) % 2, src_id % 2
    lane = lax.broadcasted_iota(jnp.int32, (1, full_tiles), 1)
    live = lane < count

    def ordered(key, code):
        tall = jnp.broadcast_to(key, (full_tiles, full_tiles)).T
        rank = jnp.sum(jnp.where(tall < key, 1, 0), axis=0, keepdims=True)
        spot = jnp.broadcast_to(rank, (full_tiles, full_tiles)).T
        tall_code = jnp.broadcast_to(code, (full_tiles, full_tiles)).T
        return jnp.sum(jnp.where(spot == lane, tall_code, 0), axis=0, keepdims=True)

    def how_many(mask):
        return jnp.sum(jnp.where(mask, 1, 0), axis=1, keepdims=True)

    row = ent_ref[0:1, :] & 15
    col = ent_ref[1:2, :] >> 4
    q = (my_x - (row & 3)) & 3
    p = my_z ^ (row >> 2)
    h = ((col >> 1) & 1) ^ my_h
    c = (col & 1) ^ my_c
    turn = (my_y - (col >> 2)) & 3
    yat = (turn ^ (turn >> 1)) * 4 + c * 2 + h
    dy = (col >> 2) ^ my_y
    spot = h * 8 + c * 4 + (dy ^ (dy >> 1))
    stage = jnp.where(q == 2, 1, 0)
    code = row + spot * 16 + (q * 4 + p) * 256 + yat * 4096
    code = ordered(jnp.where(live, stage, 3) * 128 + lane, jnp.where(live, code, 0))
    far = (code & 128) != 0
    code_b = (code & 127) + lane * 256
    code_b = ordered(jnp.where(live, jnp.where(far, 0, 1), 2) * 128 + lane, code_b)
    out_ref[0:1, :] = code
    out_ref[1:2, :] = code_b
    first = how_many(live & (stage == 0))
    away = how_many(live & far)
    out_ref[2:3, :] = jnp.where(lane == 0, first, jnp.where(lane == 2, away, count))
    out_ref[3:8, :] = jnp.zeros((5, full_tiles), jnp.int32)


def pack(count, entries, x, y, g, lw):
    return pl.pallas_call(
        pack_kernel,
        out_shape=(
            pltpu.VMEM((ROWS, BLOCK), jnp.float32), pltpu.VMEM((FEAT, BLOCK), jnp.float32),
            pltpu.VMEM((1, BLOCK), jnp.float32), pltpu.VMEM((1, BLOCK), jnp.float32), pltpu.VMEM((1, BLOCK), jnp.float32),
            pltpu.VMEM((8, full_tiles), jnp.int32),
        ),
        in_specs=[vmem] * 6,
        out_specs=[vmem] * 6,
        name="pack",
    )(count.reshape(1, 1), entries.T, x, y, g.reshape(1, BLOCK), lw.reshape(1, BLOCK))


def prepare_source(x, at, xa):
    x = x * (8.0 * log2e)
    hi = x.astype(jnp.bfloat16)
    lo = (x - hi.astype(jnp.float32)).astype(jnp.bfloat16)
    xa[at, 0:64, :] = hi
    xa[at, 64:128, :] = lo
    xa[at, 128:192, :] = hi
    xa[at, 192:256, :] = lo


def mean_square(block):
    mean = jnp.sum(block, axis=1, keepdims=True) * (1.0 / BLOCK)
    return jnp.sum(mean * mean, axis=0, keepdims=True)


def visit_tiles(unroll, plan_ref, begin, end, xa, ya, ub, k_ref, acc_ref):
    def group(step, carry):
        for u in range(unroll):
            raw = begin + step * unroll + u
            slot = jnp.minimum(raw, end - 1)
            code = plan_ref[0, slot]
            xat = (code >> 8) & 15
            yat = (code >> 12) & 15
            row = code & 15
            scores = jnp.dot(ya[yat], xa[xat], preferred_element_type=jnp.float32)
            tile = jnp.exp2(scores)
            k_ref[slot] = tile.astype(jnp.bfloat16)
            weight = ub[yat]
            left = jnp.sum((tile[:, 0:128] * weight).reshape(32, 8, 128), axis=0)
            right = jnp.sum((tile[:, 128:256] * weight).reshape(32, 8, 128), axis=0)
            live = raw < end
            acc_ref[row, :, 0:128] += jnp.where(live, left, 0.0)
            acc_ref[row, :, 128:256] += jnp.where(live, right, 0.0)
        return carry

    lax.fori_loop(0, pl.cdiv(end - begin, unroll), group, 0)


def first_kernel(
    plan_ref, x0, x1, x3, y0, z0, y1, z1, y2, z2, y3, z3,
    ya, ub, k_ref, acc_ref, stat_ref, xa, codes, sem,
):
    fetch = pltpu.make_async_copy(plan_ref, codes, sem)
    fetch.start()
    ys = (y0, z0, y1, z1, y2, z2, y3, z3)
    lines = [ys[at // 2][at % 2, FEAT : FEAT + 1, :] for at in range(SIDE)]
    top = jnp.max(functools.reduce(jnp.maximum, lines), axis=1, keepdims=True)
    low = jnp.min(functools.reduce(jnp.minimum, lines), axis=1, keepdims=True) - top
    y_sq = jnp.zeros((1, BLOCK), jnp.float32)
    for at in range(SIDE):
        y = ys[at // 2][at % 2, 0:FEAT, :]
        y_sq = jnp.maximum(y_sq, jnp.sum(y * y, axis=0, keepdims=True))
        turned = jnp.concatenate([y, y], axis=0).T
        hi = turned.astype(jnp.bfloat16)
        lo = (turned - hi.astype(jnp.float32)).astype(jnp.bfloat16)
        ya[at, :, 0:128] = hi
        ya[at, :, 128:256] = lo
        ub[at] = jnp.broadcast_to(jnp.exp2(lines[at] - top), (128, BLOCK)).T
    stat_ref[0:1, :] = jnp.broadcast_to(low, (1, BLOCK))
    stat_ref[1:2, :] = jnp.broadcast_to(top, (1, BLOCK))
    stat_ref[2:3, :] = y_sq
    x_mean = jnp.zeros((1, 1), jnp.float32)
    for q, ref in ((0, x0), (1, x1), (3, x3)):
        for p in range(4):
            block = ref[p]
            prepare_source(block, q * 4 + p, xa)
            x_mean = jnp.maximum(x_mean, mean_square(block))
    stat_ref[3:4, :] = jnp.broadcast_to(x_mean, (1, BLOCK))
    stat_ref[4:8, :] = jnp.zeros((4, BLOCK), jnp.float32)
    acc_ref[...] = jnp.zeros_like(acc_ref)
    fetch.wait()
    visit_tiles(2 * UNROLL, codes, 0, codes[2, 0], xa, ya, ub, k_ref, acc_ref)


def second_kernel(
    plan_ref, x2, ya, ub, k_in, acc_in, stat_ref, lw_ref, k_ref, s_ref, xa, acc, codes, sem
):
    fetch = pltpu.make_async_copy(plan_ref, codes, sem)
    fetch.start()
    acc[...] = acc_in[...]
    x_mean = stat_ref[3:4, 0:1]
    for p in range(4):
        block = x2[p]
        prepare_source(block, 8 + p, xa)
        x_mean = jnp.maximum(x_mean, mean_square(block))
    fetch.wait()
    visit_tiles(UNROLL, codes, codes[2, 0], codes[2, 3], xa, ya, ub, k_ref, acc)
    total = jnp.sum(acc[...], axis=1)
    low = stat_ref[0:1, 0:1]
    lean = (8.0 * log2e) * jnp.sqrt(x_mean * jnp.max(stat_ref[2:3, :], axis=1, keepdims=True))
    most = jnp.max(jnp.max(total, axis=0, keepdims=True), axis=1, keepdims=True)
    good = (lean <= 24.0) & (low >= -105.0) & (most <= jnp.exp2(120.0 + low))
    s_ref[0:16, :] = jnp.where(good, total, jnp.nan)
    s_ref[16:17, :] = stat_ref[1:2, :]
    s_ref[17:18, :] = stat_ref[1:2, :]
    s_ref[18:19, :] = lw_ref[...]
    s_ref[19:24, :] = jnp.zeros((5, BLOCK), jnp.float32)


tiles_shape = pltpu.VMEM((full_tiles, BLOCK, BLOCK), jnp.bfloat16)
target_shape = pltpu.VMEM((SIDE, BLOCK, BLOCK), jnp.bfloat16)
weight_shape = pltpu.VMEM((SIDE, BLOCK, 128), jnp.float32)
row_cost = dict(flops=32 * 2 * BLOCK**3, bytes_accessed=1 << 20, transcendentals=32 * BLOCK * BLOCK)


codes_scratch = [pltpu.SMEM((8, full_tiles), jnp.int32), pltpu.SemaphoreType.DMA]


def source_scratch(blocks):
    return pltpu.VMEM((blocks, BLOCK, BLOCK), jnp.bfloat16)


def first_pass(order, xs, ys):
    return pl.pallas_call(
        first_kernel,
        out_shape=(
            target_shape, weight_shape, tiles_shape,
            f32(SIDE, 8, BLOCK), f32(8, BLOCK),
        ),
        in_specs=[vmem] * 12,
        out_specs=[vmem] * 5,
        scratch_shapes=[source_scratch(SIDE), *codes_scratch],
        compiler_params=pltpu.CompilerParams(vmem_limit_bytes=vmem_bytes),
        cost_estimate=pl.CostEstimate(**row_cost),
        name="row_pass_a",
    )(order, *xs, *ys)


def second_pass(order, x2, ya, ub, tiles, acc, stat, lw):
    return pl.pallas_call(
        second_kernel,
        out_shape=(tiles_shape, f32(24, BLOCK)),
        in_specs=[vmem] * 8,
        out_specs=[vmem] * 2,
        scratch_shapes=[source_scratch(SIDE), pltpu.VMEM((SIDE, 8, BLOCK), jnp.float32), *codes_scratch],
        input_output_aliases={4: 0},
        compiler_params=pltpu.CompilerParams(vmem_limit_bytes=vmem_bytes),
        cost_estimate=pl.CostEstimate(**row_cost),
        name="row_pass_b",
    )(order, x2, ya, ub, tiles, acc, stat, lw)


def visit_columns(plan_ref, begin, end, v_ref, k_ref, t_ref, acc):
    acc[...] = jnp.zeros_like(acc)

    def group(step, carry):
        for u in range(UNROLL):
            raw = begin + step * UNROLL + u
            code = plan_ref[1, jnp.minimum(raw, end - 1)]
            v = jnp.where(raw < end, v_ref[pl.ds(code & 15, 1), :], 0.0)
            tile = k_ref[code >> 8].astype(jnp.float32)
            acc[(code >> 4) & 7] += tile[:, 0:128] * v[:, 0:128] + tile[:, 128:256] * v[:, 128:256]
        return carry

    lax.fori_loop(0, pl.cdiv(end - begin, UNROLL), group, 0)
    ones = jnp.ones((16, 128), jnp.bfloat16)
    across = (((1,), (1,)), ((), ()))
    for c in range(8):
        rest = acc[c]
        total = jnp.zeros((16, BLOCK), jnp.float32)
        for _ in range(3):
            part = rest.astype(jnp.bfloat16)
            rest = rest - part.astype(jnp.float32)
            total += lax.dot_general(ones, part, across, preferred_element_type=jnp.float32)
        t_ref[c : c + 1, :] = total[0:1, :]


def far_kernel(
    plan_ref, s_ref, ends_ref, lw_ref, stat_ref, xsq_ref, k_ref, f_ref, v_ref, t_ref, acc, codes, sem
):
    fetch = pltpu.make_async_copy(plan_ref, codes, sem)
    fetch.start()
    total = s_ref[...]
    shift = ends_ref[0:1, :]
    own = lax.axis_index("tgt")
    for r in range(SIDE):
        off = (r // 4) * 4 + (0, 3, 1, 2)[r % 4]
        v_ref[pl.ds(own ^ off, 1), :] = lw_ref[r : r + 1, :]
    v = jnp.exp(v_ref[...]) / total * jnp.exp2(stat_ref[1:2, :] - shift)
    fine = (total >= 1.5e-11) & (total <= 4.3e12) & (shift - ends_ref[1:2, :] <= 16.0)
    fine = jnp.where(fine, 1.0, 0.0)
    fine = jnp.min(jnp.min(fine, axis=1, keepdims=True), axis=0, keepdims=True) > 0.5
    v_ref[...] = jnp.where(fine, v, jnp.nan)
    own_s = s_ref[pl.ds(own, 1), :]
    f_ref[...] = epsilon * lw_ref[0:1, :] - epsilon * (jnp.log(own_s) + ln2 * shift) + xsq_ref[...]
    fetch.wait()
    visit_columns(codes, 0, codes[2, 2], v_ref, k_ref, t_ref, acc)
    t_ref[...] += jnp.where(fine, 0.0, jnp.nan)


def near_kernel(plan_ref, v_ref, k_ref, t_ref, acc, codes, sem):
    fetch = pltpu.make_async_copy(plan_ref, codes, sem)
    fetch.start()
    fetch.wait()
    visit_columns(codes, codes[2, 2], codes[2, 3], v_ref, k_ref, t_ref, acc)


def far_pass(order, total, ends, lw, stat, xsq, tiles):
    return pl.pallas_call(
        far_kernel,
        out_shape=(f32(1, BLOCK), f32(SIDE, BLOCK), f32(8, BLOCK)),
        in_specs=[vmem] * 7,
        out_specs=[vmem] * 3,
        scratch_shapes=[pltpu.VMEM((8, BLOCK, 128), jnp.float32), *codes_scratch],
        compiler_params=pltpu.CompilerParams(vmem_limit_bytes=vmem_bytes),
        cost_estimate=pl.CostEstimate(**row_cost),
        name="col_pass_a",
    )(order, total, ends, lw, stat, xsq, tiles)


def near_pass(order, v, tiles):
    return pl.pallas_call(
        near_kernel,
        out_shape=f32(8, BLOCK),
        in_specs=[vmem] * 3,
        out_specs=vmem,
        scratch_shapes=[pltpu.VMEM((8, BLOCK, 128), jnp.float32), *codes_scratch],
        compiler_params=pltpu.CompilerParams(vmem_limit_bytes=vmem_bytes),
        cost_estimate=pl.CostEstimate(**row_cost),
        name="col_pass_b",
    )(order, v, tiles)


def ring(k):
    return [(i, (i // 4) * 4 + (i + k) % 4) for i in range(SIDE)]


def hop(k):
    return [(i, (i + 4 * k) % SIDE) for i in range(SIDE)]


def swap(bits):
    return [(i, i ^ bits) for i in range(SIDE)]


def stacked(rows, *pieces):
    out, at = 0.0, 0
    for piece in pieces:
        height = piece.shape[0]
        out = out + lax.pad(piece, jnp.float32(0.0), ((at, rows - at - height, 0), (0, 0, 0)))
        at += height
    return out


def one_scale(*parts_weights):
    *parts, weights = parts_weights
    high = functools.reduce(jnp.maximum, [p[16:17] for p in parts])
    low = functools.reduce(jnp.minimum, [p[17:18] for p in parts])
    scaled = lax.optimization_barrier([p[0:16] * jnp.exp2(p[16:17] - high) for p in parts])
    return scaled, stacked(2, high, low), stacked(4 * weights, *[p[18 : 18 + weights] for p in parts])


def fast_form(x, y, lw, g, entries, count):
    yp, own_x, x_sq, y_sq, lw, order = pack(count, entries, x, y, g, lw)
    xz = jnp.stack([own_x] + [lax.ppermute(x, "tgt", swap(4 * k)) for k in (1, 2, 3)])
    yh = jnp.stack([yp, lax.ppermute(yp, "src", swap(2))])
    x1 = lax.ppermute(xz, "tgt", ring(1))
    x3 = lax.ppermute(xz, "tgt", ring(3))
    yy = [yh] + [lax.ppermute(yh, "src", hop(k)) for k in (1, 3, 2)]
    x2 = lax.ppermute(x1, "tgt", ring(1))
    ys = [z for a in yy for z in (a, lax.ppermute(a, "src", swap(1)))]

    ya, ub, tiles, acc, stat = first_pass(order, (xz, x1, x3), ys)
    tiles, total = second_pass(order, x2, ya, ub, tiles, acc, stat, lw)

    one, two, three = [lax.ppermute(total, "tgt", swap(k)) for k in (1, 2, 3)]
    (a, d, b, c), ends, logs = one_scale(total, three, one, two, 1)
    total = stacked(24, (d + b) + (a + c), ends, logs)
    one, two, three = [lax.ppermute(total, "tgt", swap(4 * k)) for k in (1, 2, 3)]
    (a, b, c, d), ends, logs = one_scale(total, one, two, three, 4)
    total = (b + c) + (a + d)

    f_own, v, away = far_pass(order, total, ends, logs, stat, x_sq, tiles)
    from_far = lax.ppermute(away, "src", swap(2))
    part = near_pass(order, v, tiles) + from_far
    part = part[0:4] + lax.ppermute(part[4:8], "src", swap(1))
    one, other, across = [
        lax.ppermute(part[k : k + 1], "src", swap(bits)) for k, bits in ((1, 4), (2, 12), (3, 8))
    ]
    part = (part[0:1] + one) + (other + across)
    offset = epsilon * ln2 * stat[1] + y_sq.reshape(BLOCK)
    return f_own.reshape(BLOCK), part.reshape(BLOCK), offset


def on_device(
    source_points, target_points, source_logw, target_logw, potential_in, pair_list, pair_counts
):
    f_own, t_own, offset = fast_form(
        source_points, target_points, source_logw, potential_in, pair_list[0], pair_counts
    )
    g_own = epsilon * target_logw - epsilon * jnp.log(t_own) + offset
    out_of_range = jnp.isnan(t_own[0])
    return lax.cond(
        out_of_range,
        plain_form,
        lambda *_: (f_own, g_own),
        source_points, target_points, source_logw, target_logw, potential_in, pair_list, pair_counts,
    )


def solution(mesh):
    return jax.shard_map(
        on_device,
        mesh=mesh,
        in_specs=(
            P(None, ("src", "tgt")),
            P(None, ("src", "tgt")),
            P(("src", "tgt")),
            P(("src", "tgt")),
            P(("src", "tgt")),
            P(("src", "tgt"), None, None),
            P(("src", "tgt")),
        ),
        out_specs=(P(("src", "tgt")), P(("src", "tgt"))),
        check_vma=False,
    )
```
